128 devices in a mesh: tile: 4 (over x), block: 32 (over y, z, core).
Axes of the slice: x: 4, y: 4, z: 4, core: 2. Of those that a mesh axis runs over, the one named last changes fastest.
Arguments:
- samples: bfloat16 [393216, 1024], P(('tile', 'block')), may hold values from -24 to 24
- shot_id: int32 [393216], P(('tile', 'block')), may hold values from 0 to 1023, as said below
- recv_id: int32 [393216], P(('tile', 'block')), may hold values from 0 to 2047, as said below
- shot_owner: int32 [1024], replicated, may hold values from 0 to 1023, as said below
- recv_owner: int32 [2048], replicated, may hold values from 0 to 2047, as said below
- counts: int32 [128], P(('tile', 'block')), may hold values from 1 to 3072, 157286 in all
Outputs:
- shot_terms: float32 [1024, 513], P(('tile', 'block'))
- receiver_terms: float32 [2048, 513], P(('tile', 'block'))
- residual: float32 [393216, 513], P(('tile', 'block'))
The draws below stay inside these ranges and needn't reach their ends.
Inputs may be any that keep to these rules, and one draw needn't show every extreme that they name: Each device's live traces fill its first counts slots; the largest count is 3072. `shot_id`: A trace slot of device d (of N devices) records a shot of one of two swaths of 56 shots: the one that starts at (d - 3) * 8 and the one that starts at (d + N / 2 - 3) * 8, counted modulo 1024; each device's slots name every shot of both swaths. `recv_id`: A trace slot of device d (of N devices) records a receiver of one of two swaths of 112 receivers: the one that starts at (d - 3) * 16 and the one that starts at (d + N / 2 - 3) * 16, counted modulo 2048; each device's slots name every receiver of both swaths. `shot_owner`: A permutation of the shot term table's rows that keeps each shot s in rows of owner s // 8. `recv_owner`: A permutation of the receiver term table's rows that keeps each receiver r in rows of owner r // 16.
All inputs are finite; a program needn't handle non-finite values.
Results may differ from the reference program's by a relative error of at most 0.0039.
Values sent between devices are 32-bit elements; how exact they have to be, the bound alone decides.
A program may use at most 128 MiB of HBM per device.

```python
import math
import jax
import jax.numpy as jnp
import numpy as np
from jax import lax

NSAMP = 1024
BINS = 513
TR_CAP = 3072
SHOT_DEV = 8
RECV_DEV = 16
REACH = 3
SWEEPS = 2
TRACES = 393216
SHOTS = 1024
RECEIVERS = 2048
N_TILE = 4
N_BLOCK = 32


def draw_samples(key, part):
    key = jax.random.fold_in(key, 11)
    key_noise, key_scale = jax.random.split(key, 2)
    noise = jax.random.normal(key_noise, (TRACES, NSAMP), jnp.float32)
    scale = jnp.exp(jax.random.uniform(key_scale, (TRACES, 1), jnp.float32, -1.0, 1.0))
    values = noise * scale
    return jnp.clip(values, -24.0, 24.0).astype(jnp.bfloat16)


def window_ids(key, owned, total):
    slots = jnp.arange(TRACES, dtype=jnp.int32)
    device = slots // TR_CAP
    within = slots % TR_CAP
    device_total = TRACES // TR_CAP
    width = (2 * REACH + 1) * owned
    picked = jax.random.randint(key, (TRACES,), 0, 2 * width, dtype=jnp.int32)
    spot = jnp.where(within < 2 * width, within, picked)
    swath = spot % 2
    offset = spot // 2
    first = device - REACH + swath * (device_total // 2)
    return (first * owned + offset) % total


def local_rows(key, owned, total):
    ids = jnp.arange(total, dtype=jnp.int32)
    scores = jax.random.randint(key, (total,), 0, 1 << 20, dtype=jnp.int32)
    combined = ids // owned * (1 << 20) + scores
    order = jnp.argsort(combined, stable=True).astype(jnp.int32)
    return jnp.zeros((total,), jnp.int32).at[order].set(ids)


def draw_shot_id(key, part):
    key = jax.random.fold_in(key, 21)
    return window_ids(key, SHOT_DEV, SHOTS)


def draw_recv_id(key, part):
    key = jax.random.fold_in(key, 22)
    return window_ids(key, RECV_DEV, RECEIVERS)


def draw_shot_owner(key, part):
    key = jax.random.fold_in(key, 23)
    return local_rows(key, SHOT_DEV, SHOTS)


def draw_recv_owner(key, part):
    key = jax.random.fold_in(key, 24)
    return local_rows(key, RECV_DEV, RECEIVERS)


def length_profile(count, total, bound, lean):
    portions = [(1 << 20) // math.isqrt(rank ** lean) + 1 for rank in range(2, count + 1)]
    rest, given = total - bound - (count - 1), [1] * (count - 1)
    while rest > 0:
        movable = [i for i in range(count - 1) if given[i] < bound]
        pool, budget = sum([portions[i] for i in movable]), rest
        for i in movable:
            extra = min(bound - given[i], max(1, budget * portions[i] // pool), rest)
            given[i] = given[i] + extra
            rest = rest - extra
    return np.array([bound] + given)


def uneven_parts(own_key, amount, total, reach, slope):
    if amount == 2:
        one = jax.random.randint(own_key, (), max(1, total - reach), min(reach, total - 1) + 1)
        return jnp.stack([one, total - one])
    tallies = jnp.asarray(length_profile(amount, total, reach, slope), jnp.int32)
    pairs = (amount - 1) // 2
    giver, receiver = tallies[1:1 + 2 * pairs:2], tallies[2:2 + 2 * pairs:2]
    slack = jnp.minimum(giver - 1, reach - receiver)
    passed = jax.random.randint(jax.random.fold_in(own_key, 1), (pairs,), 0, 1 << 20) % (slack + 1)
    tallies = tallies.at[1:1 + 2 * pairs:2].set(giver - passed).at[2:2 + 2 * pairs:2].set(receiver + passed)
    return tallies[jax.random.permutation(jax.random.fold_in(own_key, 2), amount)]


def setup_inputs(seed: int = 0) -> dict:
    seeds = jax.random.split(jax.random.key(seed), 7)
    return {
        "samples": draw_samples(jax.random.fold_in(seeds[6], 71), 0),
        "shot_id": draw_shot_id(jax.random.fold_in(seeds[6], 71), 0),
        "recv_id": draw_recv_id(jax.random.fold_in(seeds[6], 71), 0),
        "shot_owner": draw_shot_owner(jax.random.fold_in(seeds[6], 71), 0),
        "recv_owner": draw_recv_owner(jax.random.fold_in(seeds[6], 71), 0),
        "counts": uneven_parts(seeds[5], N_TILE * N_BLOCK, N_TILE * N_BLOCK * TR_CAP * 2 // 5, TR_CAP, 2).astype(jnp.int32),
    }


FLOOR = 0.05
DAMP = 1.0

def dft_basis(nsamp):
    half = nsamp // 2 + 1
    freq = jnp.arange(half, dtype=jnp.int32)
    sample = jnp.arange(nsamp, dtype=jnp.int32)
    phase = sample[:, None] * freq[None, :] % nsamp
    angle = phase.astype(jnp.float32) * (2.0 * math.pi / nsamp)
    norm = 1.0 / math.sqrt(nsamp)
    basis = jnp.concatenate([jnp.cos(angle) * norm, -jnp.sin(angle) * norm], axis=1)
    return basis.astype(jnp.bfloat16)

def reference(samples, shot_id, recv_id, shot_owner, recv_owner, counts):
    devices = counts.shape[0]
    rows = samples.shape[0] // devices
    nshots = shot_owner.shape[0]
    nrecv = recv_owner.shape[0]
    basis = dft_basis(NSAMP)

    def log_spectrum(block):
        spectrum = jnp.dot(block, basis, preferred_element_type=jnp.float32)
        real_part = spectrum[:, :BINS]
        imag_part = spectrum[:, BINS:]
        return jnp.log(real_part * real_part + imag_part * imag_part + FLOOR)
    log_power = lax.map(log_spectrum, samples.reshape(devices, rows, NSAMP))
    slot_index = jnp.arange(rows, dtype=jnp.int32)
    live = (slot_index[None, :] < counts[:, None]).astype(jnp.float32)
    shot_row = jnp.take(shot_owner, shot_id).astype(jnp.int32).reshape(devices, rows)
    recv_row = jnp.take(recv_owner, recv_id).astype(jnp.int32).reshape(devices, rows)
    shot_count = jax.ops.segment_sum(live.reshape(-1), shot_row.reshape(-1), num_segments=nshots)
    receiver_count = jax.ops.segment_sum(live.reshape(-1), recv_row.reshape(-1), num_segments=nrecv)
    receiver_terms = jnp.zeros((nrecv, BINS), jnp.float32)
    shot_terms = jnp.zeros((nshots, BINS), jnp.float32)
    for sweep in range(SWEEPS):

        def shot_part(carry, inputs):
            spec, alive, srow, rrow = inputs
            resid = alive[:, None] * (spec - jnp.take(receiver_terms, rrow, axis=0))
            return (carry + jax.ops.segment_sum(resid, srow, num_segments=nshots), None)
        totals, unused = lax.scan(shot_part, jnp.zeros((nshots, BINS), jnp.float32), (log_power, live, shot_row, recv_row))
        shot_terms = totals / (shot_count[:, None] + DAMP)

        def recv_part(carry, inputs):
            spec, alive, srow, rrow = inputs
            resid = alive[:, None] * (spec - jnp.take(shot_terms, srow, axis=0))
            return (carry + jax.ops.segment_sum(resid, rrow, num_segments=nrecv), None)
        totals, unused = lax.scan(recv_part, jnp.zeros((nrecv, BINS), jnp.float32), (log_power, live, shot_row, recv_row))
        receiver_terms = totals / (receiver_count[:, None] + DAMP)

    def final_rows(inputs):
        spec, alive, srow, rrow = inputs
        return alive[:, None] * (spec - jnp.take(shot_terms, srow, axis=0) - jnp.take(receiver_terms, rrow, axis=0))
    residual = lax.map(final_rows, (log_power, live, shot_row, recv_row))
    return (shot_terms, receiver_terms, residual.reshape(devices * rows, BINS))
```

```python
import functools
import math

import jax
import jax.numpy as jnp
import ml_dtypes
import numpy as np
from jax import lax
from jax.experimental import pallas as pl
from jax.experimental.pallas import tpu as pltpu
from jax.sharding import PartitionSpec as P

FLOOR = 0.05
DAMP = 1.0

GROUPS = 32
SHOT = 32
RECV = 64
REACH = 3
MSG = SHOT + RECV + 8
SMSG = SHOT + 8
RMSG = RECV + 8
TILE = 512
MESH = pl.DeviceIdType.MESH
F32 = jnp.float32
BF16 = jnp.bfloat16
HIGH = lax.Precision.HIGHEST
NT = (((1,), (1,)), ((), ()))


def basis_table(nsamp):
    half = nsamp // 2
    freq = np.arange(half + 1, dtype=np.int64)
    sample = np.arange(nsamp, dtype=np.int64)
    phase = sample[:, None] * freq[None, :] % nsamp
    angle = phase.astype(np.float32) * np.float32(2.0 * math.pi / nsamp)
    norm = np.float32(1.0 / math.sqrt(nsamp))
    cos = (np.cos(angle) * norm).astype(ml_dtypes.bfloat16)
    sin = (-np.sin(angle) * norm).astype(ml_dtypes.bfloat16)
    odd = float(sin[1, half])
    sine = sin[:, :half].copy()
    sine[:, 0] = cos[:, half]
    parts = []
    for k in range(0, half, 128):
        parts += [cos[:, k : k + 128], sine[:, k : k + 128]]
    return np.concatenate(parts, axis=1), odd


def place():
    d = lax.axis_index("tile") * 32 + lax.axis_index("block")
    return d, d // 64, (d % 64) // 2, d % 2


def device(side, group, core):
    return side * 64 + 2 * lax.rem(group + GROUPS, GROUPS) + core


def coords(d):
    return (d // 32, lax.rem(d, 32))


def local_rows(ident, live, group, core, owned):
    half = owned // 2
    total = half * GROUPS
    side = ident // total
    within = ident & (total - 1)
    j = (within // half - (group - 2 + core) + 2 * GROUPS) & (GROUPS - 1)
    row = side * half + (within & (half - 1))
    return jnp.where(live, j, -1), row


def split(x):
    hi = x.astype(BF16)
    return hi, (x - hi.astype(F32)).astype(BF16)


def solve_kernel(
    odd, shot_ref, recv_ref, count_ref, samples, basis, spec_out, table,
    x, b, w, spec, acc, cacc, racc, msgs, cmsg, inbox, cin, cg, csr, crs,
    s1, r1, s2, r2, in_sem, b_sem, out_sem, c_send, c_recv, g_send, g_recv,
    p_send, p_recv, s1_send, s1_recv, r1_send, r1_recv, s2_send, s2_recv,
    ts_send, ts_recv, tr_send, tr_recv,
):
    me, side, group, core = place()
    s = 2 * side + core
    rows = x.shape[0]
    tiles = rows // TILE

    def member(st, g):
        return device(st // 2, g, lax.rem(st, 2))

    def window_peer(n):
        j, st = n // 4, lax.rem(n, 4)
        return member(st, group + 2 - lax.rem(st, 2) - j)

    def remote(src, dst, send, recv, target):
        return pltpu.make_async_remote_copy(
            src_ref=src, dst_ref=dst, send_sem=send, recv_sem=recv,
            device_id=coords(target), device_id_type=MESH,
        )

    barrier = pltpu.get_barrier_semaphore()

    def greet(n, _):
        off, st = n // 4 - 2, lax.rem(n, 4)
        other = member(st, group + off)

        @pl.when(other != me)
        def _():
            pl.semaphore_signal(barrier, inc=1, device_id=coords(other), device_id_type=MESH)

        return 0

    lax.fori_loop(0, 20, greet, 0)
    for off in (-REACH, REACH):
        pl.semaphore_signal(
            barrier, inc=1, device_id=coords(member(s, group + off)), device_id_type=MESH
        )

    def load(i):
        part = pl.ds(pl.multiple_of(i * TILE, TILE), TILE)
        return pltpu.make_async_copy(samples.at[part], x.at[part], in_sem.at[i])

    def load_basis(k):
        part = pl.ds(256 * k, 256)
        return pltpu.make_async_copy(basis.at[:, part], b.at[:, part], b_sem.at[k])

    load_basis(0).start()
    for i in range(tiles):
        load(i).start()
    for k in range(1, 4):
        load_basis(k).start()

    slot = lax.broadcasted_iota(jnp.int32, (1, rows), 1)
    live = slot < count_ref[0]
    sj, srow = local_rows(shot_ref[...], live, group, core, SHOT)
    rj, rrow = local_rows(recv_ref[...], live, group, core, RECV)
    srow = jnp.where(live, sj * SHOT + srow, -1)
    rrow = jnp.where(live, rj * RECV + rrow, -1)
    for i in range(tiles):
        cols = slice(i * TILE, (i + 1) * TILE)
        ident = lax.broadcasted_iota(jnp.int32, (4 * SHOT, TILE), 0)
        w[: 4 * SHOT, cols] = (ident == srow[:, cols]).astype(F32).astype(BF16)
        ident = lax.broadcasted_iota(jnp.int32, (4 * RECV, TILE), 0)
        w[4 * SHOT :, cols] = (ident == rrow[:, cols]).astype(F32).astype(BF16)
    cacc[...] = jnp.zeros_like(cacc)
    racc[...] = jnp.zeros_like(racc)

    def tally(i, _):
        part = pl.ds(pl.multiple_of(i * TILE, TILE), TILE)
        ws, wr = w[: 4 * SHOT, part], w[4 * SHOT :, part]
        cacc[...] += lax.dot_general(ws, wr, NT, preferred_element_type=F32)
        racc[...] += lax.dot_general(wr, ws, NT, preferred_element_type=F32)
        return 0

    lax.fori_loop(0, tiles, tally, 0)
    for j in range(4):
        for st in range(4):
            top = j * SHOT + 8 * st
            cmsg[j, st, 0:8] = cacc[top : top + 8, 0:128]
            cmsg[j, st, 8:16] = cacc[top : top + 8, 128:256]
            top = j * RECV + 16 * st
            cmsg[j, st, 16:32] = racc[top : top + 16, :]
    csr[...] = jnp.zeros_like(csr)
    crs[...] = jnp.zeros_like(crs)
    pl.semaphore_wait(barrier, 21)

    def count_copy(n):
        j, st = n // 4, lax.rem(n, 4)
        target = member(st, group - 2 + core + j)
        return target, remote(
            cmsg.at[j, st], cin.at[4 * j + s], c_send.at[n], c_recv.at[4 * j + s], target
        )

    def send_count(n, _):
        target, copy = count_copy(n)

        @pl.when(target != me)
        def _():
            copy.start()

        return 0

    lax.fori_loop(0, 16, send_count, 0)
    cin[4 * (2 - core) + s] = cmsg[2 - core, s]

    lane = lax.broadcasted_iota(jnp.int32, (TILE, 128), 1)
    lane8 = lax.broadcasted_iota(jnp.int32, (8, 128), 1)

    def log_spectra(k):
        load_basis(k).wait()
        acc[...] = jnp.zeros_like(acc)

        def step(i, _):
            if k == 0:
                load(i).wait()
            part = pl.ds(pl.multiple_of(i * TILE, TILE), TILE)
            y = jnp.dot(x[part], b[:, 256 * k : 256 * k + 256], preferred_element_type=F32)
            re, im = y[:, :128], y[:, 128:]
            power = im * im
            if k == 0:
                power = jnp.where(lane == 0, 0.0, power)
            value = jnp.log(re * re + power + FLOOR)
            spec[k, part] = value
            pieces = list(split(value))
            if k == 0:
                re0, re512 = re[:, 0:1], im[:, 0:1]
                im512 = (odd * 16.0) * (re0 - re512)
                power = jnp.broadcast_to(re512 * re512 + im512 * im512, (TILE, 128))
                value = jnp.log(power + FLOOR)
                spec[4, part] = value
                hi, lo = split(value)
                pieces.append(jnp.where(lane == 0, hi.astype(F32), lo.astype(F32)).astype(BF16))
            width = 128 * len(pieces)
            acc[:, :width] += jnp.dot(
                w[:, part], jnp.concatenate(pieces, axis=1), preferred_element_type=F32
            )
            return 0

        lax.fori_loop(0, tiles, step, 0)
        pltpu.make_async_copy(spec.at[k], spec_out.at[k], out_sem.at[k]).start()
        for j in range(4):
            for first, size, to in ((j * SHOT, SHOT, 0), (4 * SHOT + j * RECV, RECV, SHOT)):
                msgs[k, j, to : to + size] = (
                    acc[first : first + size, 0:128] + acc[first : first + size, 128:256]
                )
        if k == 0:
            pltpu.make_async_copy(spec.at[4], spec_out.at[4], out_sem.at[4]).start()
            both = acc[:, 256:384]
            both = both + pltpu.roll(both, 127, 1)
            line = [
                jnp.broadcast_to(jnp.transpose(both[128 * v : 128 * v + 128])[0:1], (8, 128))
                for v in range(3)
            ]
            for j in range(4):
                shots = pltpu.roll(line[0], (128 - SHOT * j) % 128, 1)
                recvs = pltpu.roll(line[1 + j // 2], (SHOT + 128 - RECV * (j % 2)) % 128, 1)
                nyquist = jnp.where(lane8 < SHOT, shots, recvs)
                nyquist = jnp.where(lane8 < SHOT + RECV, nyquist, 0.0)
                for kk in range(4):
                    msgs[kk, j, SHOT + RECV : MSG] = nyquist

    def sum_copy(k, j):
        target = member(k, group - 2 + core + j)
        return target, remote(
            msgs.at[k, j], inbox.at[4 * j + s], p_send.at[4 * k + j], p_recv.at[4 * j + s], target
        )

    def send_sums(k):
        for j in range(4):
            target, copy = sum_copy(k, j)

            @pl.when(target != me)
            def _():
                copy.start()

        @pl.when(s == k)
        def _():
            inbox[4 * (2 - core) + k] = msgs[k, 2 - core]

    def arrived(buf, send, recv):
        def one(n, _):
            source = window_peer(n)

            @pl.when(source != me)
            def _():
                remote(buf.at[n], buf.at[n], send.at[n], recv.at[n], source).wait_recv()

            return 0

        lax.fori_loop(0, 16, one, 0)

    def member_copy(st):
        return remote(cg.at[s], cg.at[s], g_send.at[st], g_recv.at[s], member(st, group))

    def share_counts():
        arrived(cin, c_send, c_recv)
        shots = jnp.zeros((8, 512), F32)
        recvs = jnp.zeros((16, 256), F32)
        for j in range(4):
            part = cin[4 * j] + cin[4 * j + 1] + cin[4 * j + 2] + cin[4 * j + 3]
            wide = jnp.concatenate([part[0:8], part[8:16], jnp.zeros((8, 256), F32)], axis=1)
            shots += pltpu.roll(wide, RECV * (3 - j), 1) if j < 3 else wide
            wide = jnp.concatenate([part[16:32], jnp.zeros((16, 128), F32)], axis=1)
            recvs += pltpu.roll(wide, SHOT * (3 - j), 1) if j < 3 else wide
        for v in range(4):
            cg[s, 8 * v : 8 * v + 8] = shots[:, 128 * v : 128 * v + 128]
        for v in range(2):
            cg[s, 32 + 16 * v : 48 + 16 * v] = recvs[:, 128 * v : 128 * v + 128]
        for st in range(4):

            @pl.when(st != s)
            def _():
                member_copy(st).start()

    def take_counts():
        for st in range(4):

            @pl.when(st != s)
            def _():
                remote(
                    cg.at[st], cg.at[st], g_send.at[st], g_recv.at[st], member(st, group)
                ).wait_recv()

        for st in range(4):
            for v in range(4):
                csr[8 * st : 8 * st + 8, 128 * v : 128 * v + 128] = cg[st, 8 * v : 8 * v + 8]
            for v in range(2):
                crs[16 * st : 16 * st + 16, 128 * v : 128 * v + 128] = cg[
                    st, 32 + 16 * v : 48 + 16 * v
                ]

    log_spectra(0)
    send_sums(0)
    log_spectra(1)
    send_sums(1)
    share_counts()
    log_spectra(2)
    send_sums(2)
    take_counts()
    log_spectra(3)
    send_sums(3)

    shot_counts = jnp.sum(csr[0:SHOT], axis=1, keepdims=True) + DAMP
    recv_counts = jnp.sum(crs[0:RECV], axis=1, keepdims=True) + DAMP

    def matmul(p, q):
        return jnp.dot(p, q, precision=HIGH, preferred_element_type=F32)

    def matmul_nt(p, q):
        return lax.dot_general(p, q, NT, precision=HIGH, preferred_element_type=F32)

    shot_line = matmul_nt(jnp.ones((8, 512), F32), csr[...]) + DAMP
    recv_line = matmul_nt(jnp.ones((8, 256), F32), crs[...]) + DAMP
    for buf, size in ((s1, SMSG), (r1, RMSG), (s2, SMSG)):
        buf[7] = jnp.zeros((size, 128), F32)

    arrived(inbox, p_send, p_recv)
    total = inbox[0]
    for n in range(1, 16):
        total = total + inbox[n]
    shot_sum = total[0:SHOT]
    recv_sum = total[SHOT : SHOT + RECV]
    ends = total[SHOT + RECV : MSG]
    shot_end = jnp.where(lane8 < SHOT, ends, 0.0)
    recv_end = jnp.where(lane8 < RECV, pltpu.roll(ends, 128 - SHOT, 1), 0.0)

    def spread_copy(buf, send, recv, off):
        return remote(
            buf.at[3], buf.at[3 - off], send.at[3 - off], recv.at[3 - off], member(s, group + off)
        )

    offsets = [off for off in (3, -3, 2, -2, 1, -1)]

    def spread(buf, send, recv):
        for off in offsets:
            spread_copy(buf, send, recv, off).start()

    def gathered(buf, send, recv):
        for off in offsets:
            spread_copy(buf, send, recv, off).wait_recv()

    def shot_matrix(buf):
        main = buf[:, 0:SHOT].reshape(8 * SHOT, 128)
        line = [jnp.zeros((8, 128), F32) for _ in range(2)]
        for n in range(7):
            piece = buf[n, SHOT:SMSG]
            line[n // 4] += pltpu.roll(piece, SHOT * (n % 4), 1) if n % 4 else piece
        return main, jnp.concatenate(line, axis=1)

    def recv_matrix(buf):
        main = buf[:, 0:RECV].reshape(8 * RECV, 128)
        line = [jnp.zeros((8, 128), F32) for _ in range(4)]
        for n in range(7):
            piece = buf[n, RECV:RMSG]
            line[n // 2] += pltpu.roll(piece, RECV, 1) if n % 2 else piece
        return main, jnp.concatenate(line, axis=1)

    s1[3, 0:SHOT] = shot_sum / shot_counts
    s1[3, SHOT:SMSG] = shot_end / shot_line
    spread(s1, s1_send, s1_recv)
    gathered(s1, s1_send, s1_recv)

    main, line = shot_matrix(s1)
    r1[3, 0:RECV] = (recv_sum - matmul(crs[0:RECV], main)) / recv_counts
    r1[3, RECV:RMSG] = (recv_end - matmul_nt(line, crs[...])) / recv_line
    spread(r1, r1_send, r1_recv)
    gathered(r1, r1_send, r1_recv)

    main, line = recv_matrix(r1)
    s2[3, 0:SHOT] = (shot_sum - matmul(csr[0:SHOT], main)) / shot_counts
    s2[3, SHOT:SMSG] = (shot_end - matmul_nt(line, csr[...])) / shot_line
    spread(s2, s2_send, s2_recv)

    def table_copy(src, first, size, send, recv, n):
        j = n // 4
        return remote(
            src, table.at[s, j, pl.ds(first, size)], send.at[n], recv.at[4 * s + j], window_peer(n)
        )

    def publish(src, first, size, send, recv):
        def one(n, _):
            @pl.when(window_peer(n) != me)
            def _():
                table_copy(src, first, size, send, recv, n).start()

            return 0

        lax.fori_loop(0, 16, one, 0)

    publish(s2.at[3], 0, SMSG, ts_send, ts_recv)
    table[s, 2 - core, 0:SMSG] = s2[3]
    gathered(s2, s2_send, s2_recv)

    main, line = shot_matrix(s2)
    r2[0:RECV] = (recv_sum - matmul(crs[0:RECV], main)) / recv_counts
    r2[RECV:RMSG] = (recv_end - matmul_nt(line, crs[...])) / recv_line
    publish(r2, SMSG, RMSG, tr_send, tr_recv)
    table[s, 2 - core, SMSG : SMSG + RMSG] = r2[...]

    def drain(n, _):
        target, copy = count_copy(n)

        @pl.when(target != me)
        def _():
            copy.wait_send()

        @pl.when(window_peer(n) != me)
        def _():
            table_copy(s2.at[3], 0, SMSG, ts_send, ts_recv, n).wait_send()
            table_copy(r2, SMSG, RMSG, tr_send, tr_recv, n).wait_send()

        st, j = n // 4, lax.rem(n, 4)
        source = member(st, group - 2 + core + j)

        @pl.when(source != me)
        def _():
            for src, first, size, send, recv in (
                (s2.at[3], 0, SMSG, ts_send, ts_recv),
                (r2, SMSG, RMSG, tr_send, tr_recv),
            ):
                remote(
                    src, table.at[st, j, pl.ds(first, size)], send.at[n], recv.at[n], source
                ).wait_recv()

        return 0

    lax.fori_loop(0, 16, drain, 0)
    for k in range(4):
        for j in range(4):
            target, copy = sum_copy(k, j)

            @pl.when(target != me)
            def _():
                copy.wait_send()

        @pl.when(k != s)
        def _():
            member_copy(k).wait_send()

    for off in offsets:
        spread_copy(s1, s1_send, s1_recv, off).wait_send()
        spread_copy(r1, r1_send, r1_recv, off).wait_send()
        spread_copy(s2, s2_send, s2_recv, off).wait_send()
    for k in range(5):
        pltpu.make_async_copy(spec.at[k], spec_out.at[k], out_sem.at[k]).wait()


def solve(basis, odd, shot_id, recv_id, counts, samples):
    rows, nsamp = samples.shape
    dma = pltpu.SemaphoreType.DMA
    vmem = pl.BlockSpec(memory_space=pltpu.VMEM)
    hbm = pl.BlockSpec(memory_space=pl.ANY)
    return pl.pallas_call(
        functools.partial(solve_kernel, odd),
        out_shape=(
            jax.ShapeDtypeStruct((5, rows, 128), F32),
            jax.ShapeDtypeStruct((4, 4, SMSG + RMSG, 128), F32),
        ),
        in_specs=[vmem, vmem, pl.BlockSpec(memory_space=pltpu.SMEM), hbm, hbm],
        out_specs=(hbm, vmem),
        scratch_shapes=[
            pltpu.VMEM((rows, nsamp), BF16),
            pltpu.VMEM((nsamp, nsamp), BF16),
            pltpu.VMEM((4 * (SHOT + RECV), rows), BF16),
            pltpu.VMEM((5, rows, 128), F32),
            pltpu.VMEM((4 * (SHOT + RECV), 384), F32),
            pltpu.VMEM((4 * SHOT, 4 * RECV), F32),
            pltpu.VMEM((4 * RECV, 4 * SHOT), F32),
            pltpu.VMEM((4, 4, MSG, 128), F32),
            pltpu.VMEM((4, 4, 32, 128), F32),
            pltpu.VMEM((16, MSG, 128), F32),
            pltpu.VMEM((16, 32, 128), F32),
            pltpu.VMEM((4, 64, 128), F32),
            pltpu.VMEM((128, 8 * RECV), F32),
            pltpu.VMEM((128, 8 * SHOT), F32),
            pltpu.VMEM((8, SMSG, 128), F32),
            pltpu.VMEM((8, RMSG, 128), F32),
            pltpu.VMEM((8, SMSG, 128), F32),
            pltpu.VMEM((RMSG, 128), F32),
            dma((rows // TILE,)),
            dma((4,)),
            dma((5,)),
            dma((16,)), dma((16,)),
            dma((4,)), dma((4,)),
            dma((16,)), dma((16,)),
            dma((7,)), dma((7,)),
            dma((7,)), dma((7,)),
            dma((7,)), dma((7,)),
            dma((16,)), dma((16,)),
            dma((16,)), dma((16,)),
        ],
        compiler_params=pltpu.CompilerParams(
            collective_id=0, has_side_effects=True, vmem_limit_bytes=40 * 2**20
        ),
        cost_estimate=pl.CostEstimate(
            flops=9 * 10**9, bytes_accessed=16 * 10**6, transcendentals=2 * 10**6
        ),
    )(shot_id, recv_id, counts, samples, basis)


def residual_kernel(
    shot_ref, recv_ref, count_ref, shot_owner, recv_owner, spec, table, out, shot_out, recv_out, t
):
    step = pl.program_id(0)
    d, side, group, core = place()
    s = 2 * side + core
    size = SHOT + RECV
    half = 4 * size

    @pl.when(step == 0)
    def _():
        lane = lax.broadcasted_iota(jnp.int32, (8, 128), 1)
        lines = []
        for j in range(4):
            shots = table[0, j, SHOT:SMSG]
            recvs = pltpu.roll(table[0, j, SMSG + RECV : SMSG + RMSG], SHOT, 1)
            lines.append(jnp.where(lane < SHOT, shots, recvs)[0:1])
        lines.append(jnp.zeros((124, 128), F32))
        turned = jnp.transpose(jnp.concatenate(lines, axis=0))
        for j in range(4):
            for k in range(5):
                if k < 4:
                    value = jnp.concatenate(
                        [table[k, j, 0:SHOT], table[k, j, SMSG : SMSG + RECV]], axis=0
                    )
                else:
                    value = (pltpu.roll(turned, 128 - j, 1) if j else turned)[0:size]
                hi, lo = split(value)
                t[size * j : size * j + size, 128 * k : 128 * k + 128] = hi
                t[half + size * j : half + size * j + size, 128 * k : 128 * k + 128] = lo

        j = 2 - core
        ends_s = jnp.transpose(
            jnp.concatenate([table[0, j, SHOT:SMSG], jnp.zeros((120, 128), F32)], axis=0)
        )
        ends_r = jnp.transpose(
            jnp.concatenate([table[0, j, SMSG + RECV : SMSG + RMSG], jnp.zeros((120, 128), F32)], axis=0)
        )
        for owner, owned, first, ends, dst in (
            (shot_owner, 8, 0, ends_s, shot_out),
            (recv_owner, 16, SMSG, ends_r, recv_out),
        ):
            top = pl.multiple_of(first + owned * s, 8)
            index = lax.broadcasted_iota(jnp.int32, (owned, 1), 0)
            pieces = [table[k, j, pl.ds(top, owned)] for k in range(4)]
            end = jnp.zeros((owned, 128), F32)
            for st in range(4):
                end = jnp.where(s == st, ends[owned * st : owned * st + owned], end)
            pieces.append(end)
            for k in range(5):
                value = jnp.zeros((owned, 128), F32)
                for i in range(owned):
                    row = owner[owned * d + i] - owned * d
                    value = jnp.where(index == row, pieces[k][i : i + 1], value)
                if k < 4:
                    dst[:, 128 * k : 128 * k + 128] = value
                else:
                    dst[:, 512:513] = value[:, 0:1]

    rows = out.shape[0]
    count = count_ref[0] - step * rows

    def turned(ref, owned, to):
        live = lax.broadcasted_iota(jnp.int32, (1, rows), 1) < count
        j, row = local_rows(ref[...], live, group, core, owned)
        row = jnp.where(live, j * size + to + row, -1)
        return jnp.transpose(jnp.broadcast_to(row, (128, rows)))

    shots, recvs = turned(shot_ref, SHOT, 0), turned(recv_ref, RECV, SHOT)
    lane = lax.broadcasted_iota(jnp.int32, (rows, 128), 1)
    hot = [
        ((shots == lane + 128 * v) | (recvs == lane + 128 * v)).astype(F32).astype(BF16)
        for v in range(3)
    ]
    both = jnp.concatenate(hot + hot, axis=1)
    terms = jnp.dot(both, t[...], preferred_element_type=F32)
    live = lax.broadcasted_iota(jnp.int32, (rows, 128), 0) < count
    for k in range(4):
        part = slice(128 * k, 128 * k + 128)
        out[:, part] = jnp.where(live, spec[k], 0.0) - terms[:, part]
    out[:, 512:513] = (jnp.where(live, spec[4], 0.0) - terms[:, 512:640])[:, 0:1]


def residuals(shot_id, recv_id, counts, shot_owner, recv_owner, spec, table):
    rows = spec.shape[1]
    smem = pl.BlockSpec(memory_space=pltpu.SMEM)
    return pl.pallas_call(
        residual_kernel,
        grid=(rows // TILE,),
        out_shape=(
            jax.ShapeDtypeStruct((rows, 513), F32),
            jax.ShapeDtypeStruct((8, 513), F32),
            jax.ShapeDtypeStruct((16, 513), F32),
        ),
        in_specs=[
            pl.BlockSpec((1, TILE), lambda i: (0, i)),
            pl.BlockSpec((1, TILE), lambda i: (0, i)),
            smem,
            smem,
            smem,
            pl.BlockSpec((5, TILE, 128), lambda i: (0, i, 0)),
            pl.BlockSpec((4, 4, SMSG + RMSG, 128), lambda i: (0, 0, 0, 0)),
        ],
        out_specs=(
            pl.BlockSpec((TILE, 513), lambda i: (i, 0)),
            pl.BlockSpec((8, 513), lambda i: (0, 0)),
            pl.BlockSpec((16, 513), lambda i: (0, 0)),
        ),
        scratch_shapes=[pltpu.VMEM((8 * (SHOT + RECV), 640), BF16)],
        compiler_params=pltpu.CompilerParams(vmem_limit_bytes=32 * 2**20),
        cost_estimate=pl.CostEstimate(
            flops=3 * 10**9, bytes_accessed=16 * 10**6, transcendentals=0
        ),
    )(shot_id, recv_id, counts, shot_owner, recv_owner, spec, table)


def shards(basis, odd, samples, shot_id, recv_id, shot_owner, recv_owner, counts):
    rows = samples.shape[0]
    shot_id, recv_id = shot_id.reshape(1, rows), recv_id.reshape(1, rows)
    spec, table = solve(basis, odd, shot_id, recv_id, counts, samples)
    residual, shots, recvs = residuals(
        shot_id, recv_id, counts, shot_owner, recv_owner, spec, table
    )
    return shots, recvs, residual


def solution(mesh):
    basis, odd = basis_table(1024)

    def run(*args):
        return shards(jnp.asarray(basis), odd, *args)

    return jax.shard_map(
        run,
        mesh=mesh,
        in_specs=(
            P(("tile", "block"), None),
            P(("tile", "block")),
            P(("tile", "block")),
            P(),
            P(),
            P(("tile", "block")),
        ),
        out_specs=(
            P(("tile", "block"), None),
            P(("tile", "block"), None),
            P(("tile", "block"), None),
        ),
        check_vma=False,
    )
```

```python
import functools
import math

import jax
import jax.numpy as jnp
import ml_dtypes
import numpy as np
from jax import lax
from jax.experimental import pallas as pl
from jax.experimental.pallas import tpu as pltpu
from jax.sharding import PartitionSpec as P

FLOOR = 0.05
DAMP = 1.0

GROUPS = 32
SHOT = 32
RECV = 64
REACH = 3
MSG = SHOT + RECV + 8
SMSG = SHOT + 8
RMSG = RECV + 8
TILE = 1024
LANES = 512
MESH = pl.DeviceIdType.MESH
F32 = jnp.float32
BF16 = jnp.bfloat16
HIGH = lax.Precision.HIGHEST
NT = (((1,), (1,)), ((), ()))


def basis_table(nsamp):
    half = nsamp // 2
    freq = np.arange(half + 1, dtype=np.int64)
    sample = np.arange(nsamp, dtype=np.int64)
    phase = sample[:, None] * freq[None, :] % nsamp
    angle = phase.astype(np.float32) * np.float32(2.0 * math.pi / nsamp)
    norm = np.float32(1.0 / math.sqrt(nsamp))
    cos = (np.cos(angle) * norm).astype(ml_dtypes.bfloat16)
    sin = (-np.sin(angle) * norm).astype(ml_dtypes.bfloat16)
    odd = float(sin[1, half])
    parts = []
    for k in range(0, half, 128):
        parts += [cos[:, k : k + 128], sin[:, k : k + 128]]
    return np.concatenate(parts, axis=1), (odd, float(norm))


def place():
    d = lax.axis_index("tile") * 32 + lax.axis_index("block")
    return d, d // 64, (d % 64) // 2, d % 2


def device(side, group, core):
    return side * 64 + 2 * lax.rem(group + GROUPS, GROUPS) + core


def coords(d):
    return (d // 32, lax.rem(d, 32))


def local_rows(ident, live, group, core, owned):
    half = owned // 2
    total = half * GROUPS
    side = ident // total
    within = ident & (total - 1)
    j = (within // half - (group - 2 + core) + 2 * GROUPS) & (GROUPS - 1)
    row = side * half + (within & (half - 1))
    return jnp.where(live, j, -1), row


def split(x):
    hi = x.astype(BF16)
    return hi, (x - hi.astype(F32)).astype(BF16)


def solve_kernel(
    odd, shot_ref, recv_ref, count_ref, samples, basis, spec, w, table,
    x, b, shot_ids, recv_ids, acc, cacc, racc, msgs, cmsg, inbox, cin, cg, csr, crs,
    s1, r1, s2, r2, in_sem, b_sem, id_sem, c_send, c_recv, g_send, g_recv,
    p_send, p_recv, s1_send, s1_recv, r1_send, r1_recv, s2_send, s2_recv,
    ts_send, ts_recv, tr_send, tr_recv,
):
    me, side, group, core = place()
    s = 2 * side + core
    rows = x.shape[0]
    tiles = rows // TILE

    sides, cores = (side, 1 - side), (core, 1 - core)
    places = {}
    for off in range(-REACH, REACH + 1):
        g = lax.rem(group + (off + GROUPS), GROUPS)
        places[off] = (g // 16, 2 * lax.rem(g, 16))
    far_off = 4 * core - 2
    g = lax.rem(group + far_off + GROUPS, GROUPS)
    places["far"] = (g // 16, 2 * lax.rem(g, 16))

    def peer(off, r):
        tile, block = places[off]
        return (2 * sides[r // 2] + tile, block + cores[r % 2])

    def edge_peer(off, r1):
        tile, block = places[off]
        return (2 * sides[r1] + tile, block + (0 if off > 0 else 1))

    window = ((0, 2 - core), (-1, 1 - core), (1, 3 - core), ("far", 3 * core))

    def landing(off, r):
        if off == "far":
            return 12 + 2 * core + r // 2
        return {0: r, 1: 4 + r, -1: 8 + r}[off]

    def remote(src, dst, send, recv, target):
        return pltpu.make_async_remote_copy(
            src_ref=src, dst_ref=dst, send_sem=send, recv_sem=recv,
            device_id=target, device_id_type=MESH,
        )

    barrier = pltpu.get_barrier_semaphore()
    near = [peer(off, r) for off in range(-2, 3) for r in range(4) if (off, r) != (0, 0)]
    for target in near + [peer(-REACH, 0), peer(REACH, 0)]:
        pl.semaphore_signal(barrier, inc=1, device_id=target, device_id_type=MESH)

    def quarter(r):
        return 2 * sides[r // 2] + cores[r % 2]

    def load(i):
        part = pl.ds(pl.multiple_of(i * TILE, TILE), TILE)
        return pltpu.make_async_copy(samples.at[part], x.at[part], in_sem.at[i])

    def load_basis(n, r):
        part = pl.ds(pl.multiple_of(256 * quarter(r), 256), 256)
        return pltpu.make_async_copy(basis.at[:, part], b.at[n], b_sem.at[n])

    ids = [
        pltpu.make_async_copy(shot_ref, shot_ids, id_sem.at[0]),
        pltpu.make_async_copy(recv_ref, recv_ids, id_sem.at[1]),
    ]
    for copy in ids:
        copy.start()
    order = (3, 2, 1, 0)
    load_basis(0, order[0]).start()
    for i in range(tiles):
        load(i).start()
    for n in range(1, 4):
        load_basis(n, order[n]).start()

    for copy in ids:
        copy.wait()
    slot = lax.broadcasted_iota(jnp.int32, (1, rows), 1)
    live = slot < count_ref[0]
    sj, srow = local_rows(shot_ids[...], live, group, core, SHOT)
    rj, rrow = local_rows(recv_ids[...], live, group, core, RECV)
    srow = jnp.where(live, sj * SHOT + srow, -1)
    rrow = jnp.where(live, rj * RECV + rrow, -1)
    for i in range(tiles):
        cols = slice(i * TILE, (i + 1) * TILE)
        ident = lax.broadcasted_iota(jnp.int32, (4 * SHOT, TILE), 0)
        w[: 4 * SHOT, cols] = (ident == srow[:, cols]).astype(F32).astype(BF16)
        ident = lax.broadcasted_iota(jnp.int32, (4 * RECV, TILE), 0)
        w[4 * SHOT :, cols] = (ident == rrow[:, cols]).astype(F32).astype(BF16)
    cacc[...] = jnp.zeros_like(cacc)
    racc[...] = jnp.zeros_like(racc)

    def tally(i, _):
        part = pl.ds(pl.multiple_of(i * TILE, TILE), TILE)
        ws, wr = w[: 4 * SHOT, part], w[4 * SHOT :, part]
        cacc[...] += lax.dot_general(ws, wr, NT, preferred_element_type=F32)
        racc[...] += lax.dot_general(wr, ws, NT, preferred_element_type=F32)
        return 0

    lax.fori_loop(0, tiles, tally, 0)
    for j in range(4):
        for st in range(4):
            top = j * SHOT + 8 * st
            cmsg[j, st, 0:8] = cacc[top : top + 8, 0:128]
            cmsg[j, st, 8:16] = cacc[top : top + 8, 128:256]
            top = j * RECV + 16 * st
            cmsg[j, st, 16:32] = racc[top : top + 16, :]
    csr[...] = jnp.zeros_like(csr)
    crs[...] = jnp.zeros_like(crs)

    def count_copy(n):
        (off, j), r = window[n // 4], n % 4
        to = landing(off, r)
        return remote(
            cmsg.at[j, quarter(r)], cin.at[to], c_send.at[n], c_recv.at[to], peer(off, r)
        )

    lane = lax.broadcasted_iota(jnp.int32, (TILE, 128), 1)
    lane8 = lax.broadcasted_iota(jnp.int32, (8, 128), 1)
    sine, norm = odd

    def nyquist(i):
        part = slice(i * TILE, (i + 1) * TILE)
        even_odd = x[part, 0:128].astype(F32)
        for v in range(1, x.shape[1] // 128):
            even_odd += x[part, 128 * v : 128 * v + 128].astype(F32)
        odds = jnp.sum(jnp.where(lane % 2 == 1, even_odd, 0.0), axis=1, keepdims=True)
        evens = jnp.sum(jnp.where(lane % 2 == 1, 0.0, even_odd), axis=1, keepdims=True)
        re, im = (evens - odds) * norm, odds * sine
        return jnp.log(jnp.broadcast_to(re * re + im * im, (TILE, 128)) + FLOOR)

    def log_spectra(n):
        load_basis(n, order[n]).wait()
        first = pl.multiple_of(128 * quarter(order[n]), 128)
        acc[...] = jnp.zeros_like(acc)
        for i in range(tiles):
            if n == 0:
                load(i).wait()
            part = slice(i * TILE, (i + 1) * TILE)
            y = jnp.dot(x[part], b[n], preferred_element_type=F32)
            re, im = y[:, :128], y[:, 128:]
            value = jnp.log(re * re + im * im + FLOOR)
            spec[pl.ds(first, 128), part] = jnp.transpose(value)
            pieces = list(split(value))
            if n == 0:
                value = nyquist(i)
                spec[512:520, part] = jnp.transpose(value)[0:8]
                hi, lo = split(value)
                pieces.append(jnp.where(lane == 0, hi.astype(F32), lo.astype(F32)).astype(BF16))
            width = 128 * len(pieces)
            acc[:, :width] += jnp.dot(
                w[:, part], jnp.concatenate(pieces, axis=1), preferred_element_type=F32
            )
        for j in range(4):
            for top, size, to in ((j * SHOT, SHOT, 0), (4 * SHOT + j * RECV, RECV, SHOT)):
                msgs[n, j, to : to + size] = (
                    acc[top : top + size, 0:128] + acc[top : top + size, 128:256]
                )
        if n == 0:
            both = acc[:, 256:384]
            both = both + pltpu.roll(both, 127, 1)
            line = [
                jnp.broadcast_to(jnp.transpose(both[128 * v : 128 * v + 128])[0:1], (8, 128))
                for v in range(3)
            ]
            for j in range(4):
                shots = pltpu.roll(line[0], (128 - SHOT * j) % 128, 1)
                recvs = pltpu.roll(line[1 + j // 2], (SHOT + 128 - RECV * (j % 2)) % 128, 1)
                ends = jnp.where(lane8 < SHOT, shots, recvs)
                ends = jnp.where(lane8 < SHOT + RECV, ends, 0.0)
                for m in range(4):
                    msgs[m, j, SHOT + RECV : MSG] = ends

    def sum_copy(n, which):
        (off, j), r = window[which], order[n]
        to = landing(off, r)
        return remote(
            msgs.at[n, j], inbox.at[to], p_send.at[4 * n + which], p_recv.at[to], peer(off, r)
        )

    def sum_copies(n):
        return [sum_copy(n, which) for which in range(4) if (which, order[n]) != (0, 0)]

    def send_sums(n):
        for copy in sum_copies(n):
            copy.start()
        if order[n] == 0:
            inbox[0] = msgs[n, 2 - core]

    def senders():
        yield from ((r, peer(0, r)) for r in range(1, 4))
        for base, off in ((4, -1), (8, 1)):
            yield from ((base + r, peer(off, r)) for r in range(4))
        for base, off in ((12, 2), (14, -2)):
            yield from ((base + r1, edge_peer(off, r1)) for r1 in range(2))

    def arrived(buf, send, recv):
        for n, source in senders():
            remote(buf.at[n], buf.at[n], send.at[n], recv.at[n], source).wait_recv()

    def member_copy(r):
        return remote(cg.at[s], cg.at[s], g_send.at[r], g_recv.at[r], peer(0, r))

    def share_counts():
        arrived(cin, c_send, c_recv)
        shots = jnp.zeros((8, 512), F32)
        recvs = jnp.zeros((16, 256), F32)
        for place in range(4):
            far = {0: 14, 3: 12}
            if place in far:
                base, c = (4, core) if place == 0 else (8, 1 - core)
                part = cin[far[place]] + cin[far[place] + 1]
                part = part + cin[base + c] + cin[base + 2 + c]
            else:
                low, high = (4, 0) if place == 1 else (0, 8)
                part = cin[low + 1 - core] + cin[low + 3 - core]
                part = part + cin[high + core] + cin[high + 2 + core]
            wide = jnp.concatenate([part[0:8], part[8:16], jnp.zeros((8, 256), F32)], axis=1)
            shots += pltpu.roll(wide, RECV * place, 1) if place else wide
            wide = jnp.concatenate([part[16:32], jnp.zeros((16, 128), F32)], axis=1)
            recvs += pltpu.roll(wide, SHOT * place, 1) if place else wide
        for v in range(4):
            cg[s, 8 * v : 8 * v + 8] = shots[:, 128 * v : 128 * v + 128]
        for v in range(2):
            cg[s, 32 + 16 * v : 48 + 16 * v] = recvs[:, 128 * v : 128 * v + 128]
        for r in range(1, 4):
            member_copy(r).start()

    def take_counts():
        for r in range(1, 4):
            st = quarter(r)
            remote(cg.at[st], cg.at[st], g_send.at[r], g_recv.at[r], peer(0, r)).wait_recv()
        for st in range(4):
            for v in range(4):
                csr[8 * st : 8 * st + 8, 128 * v : 128 * v + 128] = cg[st, 8 * v : 8 * v + 8]
            for v in range(2):
                crs[16 * st : 16 * st + 16, 128 * v : 128 * v + 128] = cg[
                    st, 32 + 16 * v : 48 + 16 * v
                ]

    log_spectra(0)
    pl.semaphore_wait(barrier, 21)
    for n in range(1, 16):
        count_copy(n).start()
    cin[0] = cmsg[2 - core, s]
    send_sums(0)
    log_spectra(1)
    send_sums(1)
    share_counts()
    log_spectra(2)
    send_sums(2)
    take_counts()
    log_spectra(3)
    send_sums(3)

    shot_counts = jnp.sum(csr[0:SHOT], axis=1, keepdims=True) + DAMP
    recv_counts = jnp.sum(crs[0:RECV], axis=1, keepdims=True) + DAMP

    def matmul(p, q):
        return jnp.dot(p, q, precision=HIGH, preferred_element_type=F32)

    def matmul_nt(p, q):
        return lax.dot_general(p, q, NT, precision=HIGH, preferred_element_type=F32)

    shot_line = matmul_nt(jnp.ones((8, 512), F32), csr[...]) + DAMP
    recv_line = matmul_nt(jnp.ones((8, 256), F32), crs[...]) + DAMP
    for buf, size in ((s1, SMSG), (r1, RMSG), (s2, SMSG)):
        buf[7] = jnp.zeros((size, 128), F32)

    arrived(inbox, p_send, p_recv)
    total = inbox[0]
    for n in range(1, 16):
        total = total + inbox[n]
    shot_sum = total[0:SHOT]
    recv_sum = total[SHOT : SHOT + RECV]
    ends = total[SHOT + RECV : MSG]
    shot_end = jnp.where(lane8 < SHOT, ends, 0.0)
    recv_end = jnp.where(lane8 < RECV, pltpu.roll(ends, 128 - SHOT, 1), 0.0)

    def spread_copy(buf, send, recv, off):
        return remote(
            buf.at[3], buf.at[3 - off], send.at[3 - off], recv.at[3 - off], peer(off, 0)
        )

    offsets = (3, -3, 2, -2, 1, -1)

    def spread(buf, send, recv):
        for off in offsets:
            spread_copy(buf, send, recv, off).start()

    def gathered(buf, send, recv):
        for off in offsets:
            spread_copy(buf, send, recv, off).wait_recv()

    def shot_matrix(buf):
        main = buf[:, 0:SHOT].reshape(8 * SHOT, 128)
        line = [jnp.zeros((8, 128), F32) for _ in range(2)]
        for n in range(7):
            piece = buf[n, SHOT:SMSG]
            line[n // 4] += pltpu.roll(piece, SHOT * (n % 4), 1) if n % 4 else piece
        return main, jnp.concatenate(line, axis=1)

    def recv_matrix(buf):
        main = buf[:, 0:RECV].reshape(8 * RECV, 128)
        line = [jnp.zeros((8, 128), F32) for _ in range(4)]
        for n in range(7):
            piece = buf[n, RECV:RMSG]
            line[n // 2] += pltpu.roll(piece, RECV, 1) if n % 2 else piece
        return main, jnp.concatenate(line, axis=1)

    s1[3, 0:SHOT] = shot_sum / shot_counts
    s1[3, SHOT:SMSG] = shot_end / shot_line
    spread(s1, s1_send, s1_recv)
    gathered(s1, s1_send, s1_recv)

    main, line = shot_matrix(s1)
    r1[3, 0:RECV] = (recv_sum - matmul(crs[0:RECV], main)) / recv_counts
    r1[3, RECV:RMSG] = (recv_end - matmul_nt(line, crs[...])) / recv_line
    spread(r1, r1_send, r1_recv)
    gathered(r1, r1_send, r1_recv)

    main, line = recv_matrix(r1)
    s2[3, 0:SHOT] = (shot_sum - matmul(csr[0:SHOT], main)) / shot_counts
    s2[3, SHOT:SMSG] = (shot_end - matmul_nt(line, csr[...])) / shot_line
    spread(s2, s2_send, s2_recv)

    def publications(src, first, size, send, recv):
        rows = pl.ds(first, size)
        for off in (0, -1, 1):
            for r in range(4):
                if (off, r) != (0, 0):
                    n = {0: 0, -1: 8, 1: 4}[off] + r
                    j = 2 - off - cores[r % 2]
                    yield remote(src, table.at[s, j, rows], send.at[n], recv.at[n], peer(off, r))
        for r1 in range(2):
            for n, off, j, c in ((12 + r1, 2, 0, core), (14 + r1, -2, 3, 1 - core)):
                yield remote(
                    src, table.at[s, j, rows], send.at[n], recv.at[12 + 2 * r1 + c], edge_peer(off, r1)
                )

    def publish(*what):
        for copy in publications(*what):
            copy.start()

    def published(src, first, size, send, recv):
        rows = pl.ds(first, size)
        for base, (off, j) in zip((0, 4, 8, 12), window):
            for r in range(4):
                if (off, r) != (0, 0):
                    remote(
                        src, table.at[quarter(r), j, rows], send.at[base + r], recv.at[base + r],
                        peer(off, r),
                    ).wait_recv()

    shot_terms = (s2.at[3], 0, SMSG, ts_send, ts_recv)
    recv_terms = (r2, SMSG, RMSG, tr_send, tr_recv)
    publish(*shot_terms)
    table[s, 2 - core, 0:SMSG] = s2[3]
    gathered(s2, s2_send, s2_recv)

    main, line = shot_matrix(s2)
    r2[0:RECV] = (recv_sum - matmul(crs[0:RECV], main)) / recv_counts
    r2[RECV:RMSG] = (recv_end - matmul_nt(line, crs[...])) / recv_line
    publish(*recv_terms)
    table[s, 2 - core, SMSG : SMSG + RMSG] = r2[...]

    for n in range(1, 16):
        count_copy(n).wait_send()
    for n in range(4):
        for copy in sum_copies(n):
            copy.wait_send()
    for r in range(1, 4):
        member_copy(r).wait_send()
    for off in offsets:
        spread_copy(s1, s1_send, s1_recv, off).wait_send()
        spread_copy(r1, r1_send, r1_recv, off).wait_send()
        spread_copy(s2, s2_send, s2_recv, off).wait_send()
    for what in (shot_terms, recv_terms):
        for copy in publications(*what):
            copy.wait_send()
    for what in (shot_terms, recv_terms):
        published(*what)


def solve(basis, odd, shot_id, recv_id, counts, samples):
    rows, nsamp = samples.shape
    dma = pltpu.SemaphoreType.DMA
    vmem = pl.BlockSpec(memory_space=pltpu.VMEM)
    hbm = pl.BlockSpec(memory_space=pltpu.HBM)
    return pl.pallas_call(
        functools.partial(solve_kernel, odd),
        out_shape=(
            jax.ShapeDtypeStruct((nsamp // 2 + 8, rows), F32),
            jax.ShapeDtypeStruct((4 * (SHOT + RECV), rows), BF16),
            jax.ShapeDtypeStruct((4, 4, SMSG + RMSG, 128), F32),
        ),
        in_specs=[hbm, hbm, pl.BlockSpec(memory_space=pltpu.SMEM), hbm, hbm],
        out_specs=(vmem, vmem, vmem),
        scratch_shapes=[
            pltpu.VMEM((rows, nsamp), BF16),
            pltpu.VMEM((4, nsamp, 256), BF16),
            pltpu.VMEM((1, rows), jnp.int32),
            pltpu.VMEM((1, rows), jnp.int32),
            pltpu.VMEM((4 * (SHOT + RECV), 384), F32),
            pltpu.VMEM((4 * SHOT, 4 * RECV), F32),
            pltpu.VMEM((4 * RECV, 4 * SHOT), F32),
            pltpu.VMEM((4, 4, MSG, 128), F32),
            pltpu.VMEM((4, 4, 32, 128), F32),
            pltpu.VMEM((16, MSG, 128), F32),
            pltpu.VMEM((16, 32, 128), F32),
            pltpu.VMEM((4, 64, 128), F32),
            pltpu.VMEM((128, 8 * RECV), F32),
            pltpu.VMEM((128, 8 * SHOT), F32),
            pltpu.VMEM((8, SMSG, 128), F32),
            pltpu.VMEM((8, RMSG, 128), F32),
            pltpu.VMEM((8, SMSG, 128), F32),
            pltpu.VMEM((RMSG, 128), F32),
            dma((rows // TILE,)),
            dma((4,)),
            dma((2,)),
            dma((16,)), dma((16,)),
            dma((4,)), dma((4,)),
            dma((16,)), dma((16,)),
            dma((7,)), dma((7,)),
            dma((7,)), dma((7,)),
            dma((7,)), dma((7,)),
            dma((16,)), dma((16,)),
            dma((16,)), dma((16,)),
        ],
        compiler_params=pltpu.CompilerParams(
            collective_id=0, has_side_effects=True, vmem_limit_bytes=32 * 2**20
        ),
        cost_estimate=pl.CostEstimate(
            flops=9 * 10**9, bytes_accessed=16 * 10**6, transcendentals=2 * 10**6
        ),
    )(shot_id, recv_id, counts, samples, basis)


def residual_kernel(count_ref, shot_owner, recv_owner, spec, w, table, out, shot_out, recv_out, t):
    step = pl.program_id(0)
    d, side, group, core = place()
    s = 2 * side + core
    width = 4 * (SHOT + RECV)

    @pl.when(step == 0)
    def _():
        def put(first, value):
            hi, lo = split(value)
            t[first : first + value.shape[0], 0:width] = hi
            t[first : first + value.shape[0], width : 2 * width] = lo

        for k in range(4):
            shots = [table[k, j, 0:SHOT] for j in range(4)]
            recvs = [table[k, j, SMSG : SMSG + RECV] for j in range(4)]
            put(128 * k, jnp.transpose(jnp.concatenate(shots + recvs, axis=0)))
        shots = [table[0, j, SHOT:SMSG] for j in range(4)]
        recvs = [table[0, j, SMSG + RECV : SMSG + RMSG] for j in range(4)]
        line = shots[0]
        for j in range(1, 4):
            line = line + pltpu.roll(shots[j], SHOT * j, 1)
        lines = [line]
        for j in range(0, 4, 2):
            lines.append(recvs[j] + pltpu.roll(recvs[j + 1], RECV, 1))
        put(512, jnp.concatenate(lines, axis=1))

        j = 2 - core
        blank = jnp.zeros((120, 128), F32)
        ends_s = jnp.transpose(jnp.concatenate([table[0, j, SHOT:SMSG], blank], axis=0))
        ends_r = jnp.transpose(
            jnp.concatenate([table[0, j, SMSG + RECV : SMSG + RMSG], blank], axis=0)
        )
        for owner, owned, first, ends, dst in (
            (shot_owner, 8, 0, ends_s, shot_out),
            (recv_owner, 16, SMSG, ends_r, recv_out),
        ):
            top = pl.multiple_of(first + owned * s, 8)
            index = lax.broadcasted_iota(jnp.int32, (owned, 1), 0)
            pieces = [table[k, j, pl.ds(top, owned)] for k in range(4)]
            end = jnp.zeros((owned, 128), F32)
            for st in range(4):
                end = jnp.where(s == st, ends[owned * st : owned * st + owned], end)
            pieces.append(end)
            for k in range(5):
                value = jnp.zeros((owned, 128), F32)
                for i in range(owned):
                    row = owner[owned * d + i] - owned * d
                    value = jnp.where(index == row, pieces[k][i : i + 1], value)
                if k < 4:
                    dst[:, 128 * k : 128 * k + 128] = value
                else:
                    dst[:, 512:513] = value[:, 0:1]

    part = pl.ds(pl.multiple_of(step * LANES, LANES), LANES)
    hot = w[:, part]
    terms = jnp.dot(t[...], jnp.concatenate([hot, hot], axis=0), preferred_element_type=F32)
    live = lax.broadcasted_iota(jnp.int32, (1, LANES), 1) < count_ref[0] - step * LANES
    out[...] = (jnp.where(live, spec[:, part], 0.0) - terms)[0 : out.shape[0]]


def residuals(counts, shot_owner, recv_owner, spec, w, table):
    rows = spec.shape[1]
    smem = pl.BlockSpec(memory_space=pltpu.SMEM)
    vmem = pl.BlockSpec(memory_space=pltpu.VMEM)
    return pl.pallas_call(
        residual_kernel,
        grid=(rows // LANES,),
        out_shape=(
            jax.ShapeDtypeStruct((513, rows), F32),
            jax.ShapeDtypeStruct((8, 513), F32),
            jax.ShapeDtypeStruct((16, 513), F32),
        ),
        in_specs=[smem, smem, smem, vmem, vmem, vmem],
        out_specs=(
            pl.BlockSpec((513, LANES), lambda i: (0, i)),
            pl.BlockSpec((8, 513), lambda i: (0, 0)),
            pl.BlockSpec((16, 513), lambda i: (0, 0)),
        ),
        scratch_shapes=[pltpu.VMEM((520, 8 * (SHOT + RECV)), BF16)],
        compiler_params=pltpu.CompilerParams(vmem_limit_bytes=24 * 2**20),
        cost_estimate=pl.CostEstimate(
            flops=3 * 10**9, bytes_accessed=10 * 10**6, transcendentals=0
        ),
    )(counts, shot_owner, recv_owner, spec, w, table)


def shards(basis, odd, samples, shot_id, recv_id, shot_owner, recv_owner, counts):
    rows = samples.shape[0]
    shot_id, recv_id = shot_id.reshape(1, rows), recv_id.reshape(1, rows)
    shot_id, recv_id, samples, basis = (
        pltpu.with_memory_space_constraint(a, pltpu.HBM) for a in (shot_id, recv_id, samples, basis)
    )
    spec, w, table = solve(basis, odd, shot_id, recv_id, counts, samples)
    residual, shots, recvs = residuals(counts, shot_owner, recv_owner, spec, w, table)
    return shots, recvs, residual.T


def solution(mesh):
    basis, odd = basis_table(1024)

    def run(*args):
        return shards(jnp.asarray(basis), odd, *args)

    return jax.shard_map(
        run,
        mesh=mesh,
        in_specs=(
            P(("tile", "block"), None),
            P(("tile", "block")),
            P(("tile", "block")),
            P(),
            P(),
            P(("tile", "block")),
        ),
        out_specs=(
            P(("tile", "block"), None),
            P(("tile", "block"), None),
            P(("tile", "block"), None),
        ),
        check_vma=False,
    )
```

```python
import functools
import math

import jax
import jax.numpy as jnp
import ml_dtypes
import numpy as np
from jax import lax
from jax.experimental import pallas as pl
from jax.experimental.pallas import tpu as pltpu
from jax.sharding import PartitionSpec as P

FLOOR = 0.05
DAMP = 1.0

GROUPS = 32
SHOT = 32
RECV = 64
REACH = 3
MSG = SHOT + RECV + 8
SMSG = SHOT + 8
RMSG = RECV + 8
TILE = 1024
LANES = 512
MESH = pl.DeviceIdType.MESH
F32 = jnp.float32
BF16 = jnp.bfloat16
HIGH = lax.Precision.HIGHEST
NT = (((1,), (1,)), ((), ()))


def basis_table(nsamp):
    half = nsamp // 2
    freq = np.arange(half + 1, dtype=np.int64)
    sample = np.arange(nsamp, dtype=np.int64)
    phase = sample[:, None] * freq[None, :] % nsamp
    angle = phase.astype(np.float32) * np.float32(2.0 * math.pi / nsamp)
    norm = np.float32(1.0 / math.sqrt(nsamp))
    cos = (np.cos(angle) * norm).astype(ml_dtypes.bfloat16)
    sin = (-np.sin(angle) * norm).astype(ml_dtypes.bfloat16)
    odd = float(sin[1, half])
    parts = []
    for k in range(0, half, 128):
        parts += [cos[:, k : k + 128], sin[:, k : k + 128]]
    return np.concatenate(parts, axis=1), (odd, float(norm))


def place():
    d = lax.axis_index("tile") * 32 + lax.axis_index("block")
    return d, d // 64, (d % 64) // 2, d % 2


def device(side, group, core):
    return side * 64 + 2 * lax.rem(group + GROUPS, GROUPS) + core


def coords(d):
    return (d // 32, lax.rem(d, 32))


def local_rows(ident, live, group, core, owned):
    half = owned // 2
    total = half * GROUPS
    side = ident // total
    within = ident & (total - 1)
    j = (within // half - (group - 2 + core) + 2 * GROUPS) & (GROUPS - 1)
    row = side * half + (within & (half - 1))
    return jnp.where(live, j, -1), row


def split(x):
    hi = x.astype(BF16)
    return hi, (x - hi.astype(F32)).astype(BF16)


def solve_kernel(
    odd, shot_ref, recv_ref, count_ref, samples, basis, spec, w, table_s, table_r,
    x, b, shot_ids, recv_ids, hl, acc, cacc, racc, msgs, cmsg, inbox, cin, cg, csr, crs,
    s1, r1, s2, r2, in_sem, b_sem, id_sem, c_send, c_recv, g_send, g_recv,
    p_send, p_recv, s1_send, s1_recv, r1_send, r1_recv, s2_send, s2_recv,
    ts_send, ts_recv, tr_send, tr_recv, fs_send, fs_recv, fr_send, fr_recv,
):
    me, side, group, core = place()
    s = 2 * side + core
    rows = x.shape[0]
    tiles = rows // TILE

    sides, cores = (side, 1 - side), (core, 1 - core)
    places = {}
    for off in range(-REACH, REACH + 1):
        g = lax.rem(group + (off + GROUPS), GROUPS)
        places[off] = (g // 16, 2 * lax.rem(g, 16))
    far_off = 4 * core - 2
    g = lax.rem(group + far_off + GROUPS, GROUPS)
    places["far"] = (g // 16, 2 * lax.rem(g, 16))

    def peer(off, r):
        tile, block = places[off]
        return (2 * sides[r // 2] + tile, block + cores[r % 2])

    def edge_peer(off, r1):
        tile, block = places[off]
        return (2 * sides[r1] + tile, block + (0 if off > 0 else 1))

    window = ((0, 2 - core), (-1, 1 - core), (1, 3 - core), ("far", 3 * core))

    def landing(off, r):
        if off == "far":
            return 12 + 2 * core + r // 2
        return {0: r, 1: 4 + r, -1: 8 + r}[off]

    def remote(src, dst, send, recv, target):
        return pltpu.make_async_remote_copy(
            src_ref=src, dst_ref=dst, send_sem=send, recv_sem=recv,
            device_id=target, device_id_type=MESH,
        )

    barrier = pltpu.get_barrier_semaphore()
    near = [peer(off, r) for off in range(-2, 3) for r in range(4) if (off, r) != (0, 0)]
    for target in near + [peer(-REACH, 0), peer(REACH, 0)]:
        pl.semaphore_signal(barrier, inc=1, device_id=target, device_id_type=MESH)

    def quarter(r):
        return 2 * sides[r // 2] + cores[r % 2]

    def load(i):
        part = pl.ds(pl.multiple_of(i * TILE, TILE), TILE)
        return pltpu.make_async_copy(samples.at[part], x.at[part], in_sem.at[i])

    def load_basis(n, r):
        part = pl.ds(pl.multiple_of(256 * quarter(r), 256), 256)
        return pltpu.make_async_copy(basis.at[:, part], b.at[n], b_sem.at[n])

    ids = [
        pltpu.make_async_copy(shot_ref, shot_ids, id_sem.at[0]),
        pltpu.make_async_copy(recv_ref, recv_ids, id_sem.at[1]),
    ]
    for copy in ids:
        copy.start()
    order = (3, 2, 1, 0)
    load_basis(0, order[0]).start()
    for i in range(tiles):
        load(i).start()
    for n in range(1, 4):
        load_basis(n, order[n]).start()

    for copy in ids:
        copy.wait()
    slot = lax.broadcasted_iota(jnp.int32, (1, rows), 1)
    live = slot < count_ref[0]
    sj, srow = local_rows(shot_ids[...], live, group, core, SHOT)
    rj, rrow = local_rows(recv_ids[...], live, group, core, RECV)
    srow = jnp.where(live, sj * SHOT + srow, -1)
    rrow = jnp.where(live, rj * RECV + rrow, -1)
    for i in range(tiles):
        cols = slice(i * TILE, (i + 1) * TILE)
        ident = lax.broadcasted_iota(jnp.int32, (4 * SHOT, TILE), 0)
        w[: 4 * SHOT, cols] = (ident == srow[:, cols]).astype(F32).astype(BF16)
        ident = lax.broadcasted_iota(jnp.int32, (4 * RECV, TILE), 0)
        w[4 * SHOT :, cols] = (ident == rrow[:, cols]).astype(F32).astype(BF16)
    cacc[...] = jnp.zeros_like(cacc)
    racc[...] = jnp.zeros_like(racc)

    def tally(i, _):
        part = pl.ds(pl.multiple_of(i * TILE, TILE), TILE)
        ws, wr = w[: 4 * SHOT, part], w[4 * SHOT :, part]
        cacc[...] += lax.dot_general(ws, wr, NT, preferred_element_type=F32)
        racc[...] += lax.dot_general(wr, ws, NT, preferred_element_type=F32)
        return 0

    lax.fori_loop(0, tiles, tally, 0)
    for j in range(4):
        for st in range(4):
            top = j * SHOT + 8 * st
            cmsg[j, st, 0:8] = cacc[top : top + 8, 0:128]
            cmsg[j, st, 8:16] = cacc[top : top + 8, 128:256]
            top = j * RECV + 16 * st
            cmsg[j, st, 16:32] = racc[top : top + 16, :]
    csr[...] = jnp.zeros_like(csr)
    crs[...] = jnp.zeros_like(crs)

    def count_copy(n):
        (off, j), r = window[n // 4], n % 4
        to = landing(off, r)
        return remote(
            cmsg.at[j, quarter(r)], cin.at[to], c_send.at[n], c_recv.at[to], peer(off, r)
        )

    lane = lax.broadcasted_iota(jnp.int32, (TILE, 128), 1)
    lane8 = lax.broadcasted_iota(jnp.int32, (8, 128), 1)
    sine, norm = odd

    def nyquist(i):
        part = slice(i * TILE, (i + 1) * TILE)
        even_odd = x[part, 0:128].astype(F32)
        for v in range(1, x.shape[1] // 128):
            even_odd += x[part, 128 * v : 128 * v + 128].astype(F32)
        odds = jnp.sum(jnp.where(lane % 2 == 1, even_odd, 0.0), axis=1, keepdims=True)
        evens = jnp.sum(jnp.where(lane % 2 == 1, 0.0, even_odd), axis=1, keepdims=True)
        re, im = (evens - odds) * norm, odds * sine
        return jnp.log(jnp.broadcast_to(re * re + im * im, (TILE, 128)) + FLOOR)

    def log_spectra(n):
        load_basis(n, order[n]).wait()
        first = pl.multiple_of(128 * quarter(order[n]), 128)
        for i in range(tiles):
            if n == 0:
                load(i).wait()
            part = slice(i * TILE, (i + 1) * TILE)
            y = jnp.dot(x[part], b[n], preferred_element_type=F32)
            re, im = y[:, :128], y[:, 128:]
            value = jnp.log(re * re + im * im + FLOOR)
            spec[pl.ds(first, 128), part] = jnp.transpose(value)
            hl[part, 0:128], hl[part, 128:256] = split(value)
            if n == 0:
                value = nyquist(i)
                spec[512:520, part] = jnp.transpose(value)[0:8]
                hi, lo = split(value)
                hl[part, 256:384] = jnp.where(lane == 0, hi.astype(F32), lo.astype(F32)).astype(BF16)
        width = 384 if n == 0 else 256
        acc[:, :width] = jnp.dot(w[...], hl[:, :width], preferred_element_type=F32)
        for j in range(4):
            for top, size, to in ((j * SHOT, SHOT, 0), (4 * SHOT + j * RECV, RECV, SHOT)):
                msgs[n, j, to : to + size] = (
                    acc[top : top + size, 0:128] + acc[top : top + size, 128:256]
                )
        if n == 0:
            both = acc[:, 256:384]
            both = both + pltpu.roll(both, 127, 1)
            line = [
                jnp.broadcast_to(jnp.transpose(both[128 * v : 128 * v + 128])[0:1], (8, 128))
                for v in range(3)
            ]
            for j in range(4):
                shots = pltpu.roll(line[0], (128 - SHOT * j) % 128, 1)
                recvs = pltpu.roll(line[1 + j // 2], (SHOT + 128 - RECV * (j % 2)) % 128, 1)
                ends = jnp.where(lane8 < SHOT, shots, recvs)
                ends = jnp.where(lane8 < SHOT + RECV, ends, 0.0)
                for m in range(4):
                    msgs[m, j, SHOT + RECV : MSG] = ends

    def sum_copy(n, which):
        (off, j), r = window[which], order[n]
        to = landing(off, r)
        return remote(
            msgs.at[n, j], inbox.at[to], p_send.at[4 * n + which], p_recv.at[to], peer(off, r)
        )

    def sum_copies(n):
        return [sum_copy(n, which) for which in range(4) if (which, order[n]) != (0, 0)]

    def send_sums(n):
        for copy in sum_copies(n):
            copy.start()
        if order[n] == 0:
            inbox[0] = msgs[n, 2 - core]

    def senders():
        yield from ((r, peer(0, r)) for r in range(1, 4))
        for base, off in ((4, -1), (8, 1)):
            yield from ((base + r, peer(off, r)) for r in range(4))
        for base, off in ((12, 2), (14, -2)):
            yield from ((base + r1, edge_peer(off, r1)) for r1 in range(2))

    def arrived(buf, send, recv):
        for n, source in senders():
            remote(buf.at[n], buf.at[n], send.at[n], recv.at[n], source).wait_recv()

    def member_copy(r):
        return remote(cg.at[s], cg.at[s], g_send.at[r], g_recv.at[r], peer(0, r))

    def share_counts():
        arrived(cin, c_send, c_recv)
        shots = jnp.zeros((8, 512), F32)
        recvs = jnp.zeros((16, 256), F32)
        for place in range(4):
            far = {0: 14, 3: 12}
            if place in far:
                base, c = (4, core) if place == 0 else (8, 1 - core)
                part = cin[far[place]] + cin[far[place] + 1]
                part = part + cin[base + c] + cin[base + 2 + c]
            else:
                low, high = (4, 0) if place == 1 else (0, 8)
                part = cin[low + 1 - core] + cin[low + 3 - core]
                part = part + cin[high + core] + cin[high + 2 + core]
            wide = jnp.concatenate([part[0:8], part[8:16], jnp.zeros((8, 256), F32)], axis=1)
            shots += pltpu.roll(wide, RECV * place, 1) if place else wide
            wide = jnp.concatenate([part[16:32], jnp.zeros((16, 128), F32)], axis=1)
            recvs += pltpu.roll(wide, SHOT * place, 1) if place else wide
        for v in range(4):
            cg[s, 8 * v : 8 * v + 8] = shots[:, 128 * v : 128 * v + 128]
        for v in range(2):
            cg[s, 32 + 16 * v : 48 + 16 * v] = recvs[:, 128 * v : 128 * v + 128]
        for r in range(1, 4):
            member_copy(r).start()

    def take_counts():
        for r in range(1, 4):
            st = quarter(r)
            remote(cg.at[st], cg.at[st], g_send.at[r], g_recv.at[r], peer(0, r)).wait_recv()
        for st in range(4):
            for v in range(4):
                csr[8 * st : 8 * st + 8, 128 * v : 128 * v + 128] = cg[st, 8 * v : 8 * v + 8]
            for v in range(2):
                crs[16 * st : 16 * st + 16, 128 * v : 128 * v + 128] = cg[
                    st, 32 + 16 * v : 48 + 16 * v
                ]

    log_spectra(0)
    pl.semaphore_wait(barrier, 21)
    for n in range(1, 16):
        count_copy(n).start()
    cin[0] = cmsg[2 - core, s]
    send_sums(0)
    log_spectra(1)
    send_sums(1)
    log_spectra(2)
    send_sums(2)
    share_counts()
    log_spectra(3)
    send_sums(3)
    take_counts()

    shot_counts = jnp.sum(csr[0:SHOT], axis=1, keepdims=True) + DAMP
    recv_counts = jnp.sum(crs[0:RECV], axis=1, keepdims=True) + DAMP

    def matmul(p, q):
        return jnp.dot(p, q, precision=HIGH, preferred_element_type=F32)

    def matmul_nt(p, q):
        return lax.dot_general(p, q, NT, precision=HIGH, preferred_element_type=F32)

    shot_line = matmul_nt(jnp.ones((8, 512), F32), csr[...]) + DAMP
    recv_line = matmul_nt(jnp.ones((8, 256), F32), crs[...]) + DAMP
    for buf, size in ((s1, SMSG), (r1, RMSG), (s2, SMSG)):
        buf[7] = jnp.zeros((size, 128), F32)

    arrived(inbox, p_send, p_recv)
    total = inbox[0]
    for n in range(1, 16):
        total = total + inbox[n]
    shot_sum = total[0:SHOT]
    recv_sum = total[SHOT : SHOT + RECV]
    ends = total[SHOT + RECV : MSG]
    shot_end = jnp.where(lane8 < SHOT, ends, 0.0)
    recv_end = jnp.where(lane8 < RECV, pltpu.roll(ends, 128 - SHOT, 1), 0.0)

    def spread_copy(buf, send, recv, off):
        return remote(
            buf.at[3], buf.at[3 - off], send.at[3 - off], recv.at[3 - off], peer(off, 0)
        )

    offsets = (3, -3, 2, -2, 1, -1)

    def spread(buf, send, recv):
        for off in offsets:
            spread_copy(buf, send, recv, off).start()

    def gathered(buf, send, recv):
        for off in offsets:
            spread_copy(buf, send, recv, off).wait_recv()

    def shot_matrix(buf):
        main = buf[:, 0:SHOT].reshape(8 * SHOT, 128)
        line = [jnp.zeros((8, 128), F32) for _ in range(2)]
        for n in range(7):
            piece = buf[n, SHOT:SMSG]
            line[n // 4] += pltpu.roll(piece, SHOT * (n % 4), 1) if n % 4 else piece
        return main, jnp.concatenate(line, axis=1)

    def recv_matrix(buf):
        main = buf[:, 0:RECV].reshape(8 * RECV, 128)
        line = [jnp.zeros((8, 128), F32) for _ in range(4)]
        for n in range(7):
            piece = buf[n, RECV:RMSG]
            line[n // 2] += pltpu.roll(piece, RECV, 1) if n % 2 else piece
        return main, jnp.concatenate(line, axis=1)

    s1[3, 0:SHOT] = shot_sum / shot_counts
    s1[3, SHOT:SMSG] = shot_end / shot_line
    spread(s1, s1_send, s1_recv)
    gathered(s1, s1_send, s1_recv)

    main, line = shot_matrix(s1)
    r1[3, 0:RECV] = (recv_sum - matmul(crs[0:RECV], main)) / recv_counts
    r1[3, RECV:RMSG] = (recv_end - matmul_nt(line, crs[...])) / recv_line
    spread(r1, r1_send, r1_recv)
    gathered(r1, r1_send, r1_recv)

    main, line = recv_matrix(r1)
    s2[3, 0:SHOT] = (shot_sum - matmul(csr[0:SHOT], main)) / shot_counts
    s2[3, SHOT:SMSG] = (shot_end - matmul_nt(line, csr[...])) / shot_line
    spread(s2, s2_send, s2_recv)

    def publications(src, table, send, recv):
        for off in (2, -2, 1, -1, 0):
            for r in (2, 0):
                if (off, r) != (0, 0):
                    n = 5 * (r // 2) + 2 - off
                    yield remote(
                        src, table.at[core, side, 2 - off], send.at[n], recv.at[n], peer(off, r)
                    )

    def hand_on(table, send, recv, r, off):
        n = 5 * (r // 2) + 2 + off
        block = table.at[core, sides[r // 2], 2 + off]
        return remote(block, block, send.at[n], recv.at[n], peer(0, 1))

    def relay(src, table, send, recv, send_on, recv_on):
        for r in (0, 2):
            for off in (0, 1, -1, 2, -2):
                if (off, r) != (0, 0):
                    n = 5 * (r // 2) + 2 + off
                    remote(
                        src, table.at[core, sides[r // 2], 2 + off], send.at[n], recv.at[n],
                        peer(off, r),
                    ).wait_recv()
                hand_on(table, send_on, recv_on, r, off).start()

    def relayed(table, send, recv):
        for r in (0, 2):
            for off in (0, 1, -1, 2, -2):
                n = 5 * (r // 2) + 2 + off
                block = table.at[1 - core, sides[r // 2], 2 + off]
                remote(block, block, send.at[n], recv.at[n], peer(0, 1)).wait_recv()

    shot_terms = (s2.at[3], table_s, ts_send, ts_recv)
    recv_terms = (r2, table_r, tr_send, tr_recv)

    def publish(*what):
        for copy in publications(*what):
            copy.start()

    publish(*shot_terms)
    table_s[core, side, 2] = s2[3]
    gathered(s2, s2_send, s2_recv)

    main, line = shot_matrix(s2)
    r2[0:RECV] = (recv_sum - matmul(crs[0:RECV], main)) / recv_counts
    r2[RECV:RMSG] = (recv_end - matmul_nt(line, crs[...])) / recv_line
    publish(*recv_terms)
    table_r[core, side, 2] = r2[...]

    relay(*shot_terms, fs_send, fs_recv)
    relayed(table_s, fs_send, fs_recv)

    def both_parts(value):
        return jnp.concatenate(split(value), axis=1)

    lifted = []
    for k in range(4):
        terms = jnp.concatenate([table_s[k % 2, k // 2, j + core, 0:SHOT] for j in range(4)], axis=0)
        lifted.append(both_parts(jnp.transpose(terms)))
    line = table_s[0, 0, core, SHOT:SMSG]
    for j in range(1, 4):
        line = line + pltpu.roll(table_s[0, 0, j + core, SHOT:SMSG], SHOT * j, 1)
    lifted.append(both_parts(line))
    for i in range(tiles):
        part = slice(i * TILE, (i + 1) * TILE)
        hot = jnp.concatenate([w[0 : 4 * SHOT, part]] * 2, axis=0)
        for k in range(5):
            bins = slice(128 * k, min(128 * k + 128, spec.shape[0]))
            terms = jnp.dot(lifted[k], hot, preferred_element_type=F32)
            spec[bins, part] = jnp.where(live[:, part], spec[bins, part], 0.0) - terms

    for n in range(1, 16):
        count_copy(n).wait_send()
    for n in range(4):
        for copy in sum_copies(n):
            copy.wait_send()
    for r in range(1, 4):
        member_copy(r).wait_send()
    for off in offsets:
        spread_copy(s1, s1_send, s1_recv, off).wait_send()
        spread_copy(r1, r1_send, r1_recv, off).wait_send()
        spread_copy(s2, s2_send, s2_recv, off).wait_send()
    for what in (shot_terms, recv_terms):
        for copy in publications(*what):
            copy.wait_send()
    relay(*recv_terms, fr_send, fr_recv)
    for r in (0, 2):
        for off in range(-2, 3):
            hand_on(table_s, fs_send, fs_recv, r, off).wait_send()
            hand_on(table_r, fr_send, fr_recv, r, off).wait_send()
    relayed(table_r, fr_send, fr_recv)


def solve(basis, odd, shot_id, recv_id, counts, samples):
    rows, nsamp = samples.shape
    dma = pltpu.SemaphoreType.DMA
    vmem = pl.BlockSpec(memory_space=pltpu.VMEM)
    hbm = pl.BlockSpec(memory_space=pltpu.HBM)
    return pl.pallas_call(
        functools.partial(solve_kernel, odd),
        out_shape=(
            jax.ShapeDtypeStruct((nsamp // 2 + 8, rows), F32),
            jax.ShapeDtypeStruct((4 * (SHOT + RECV), rows), BF16),
            jax.ShapeDtypeStruct((2, 2, 5, SMSG, 128), F32),
            jax.ShapeDtypeStruct((2, 2, 5, RMSG, 128), F32),
        ),
        in_specs=[hbm, hbm, pl.BlockSpec(memory_space=pltpu.SMEM), hbm, hbm],
        out_specs=(vmem, vmem, vmem, vmem),
        scratch_shapes=[
            pltpu.VMEM((rows, nsamp), BF16),
            pltpu.VMEM((4, nsamp, 256), BF16),
            pltpu.VMEM((1, rows), jnp.int32),
            pltpu.VMEM((1, rows), jnp.int32),
            pltpu.VMEM((rows, 384), BF16),
            pltpu.VMEM((4 * (SHOT + RECV), 384), F32),
            pltpu.VMEM((4 * SHOT, 4 * RECV), F32),
            pltpu.VMEM((4 * RECV, 4 * SHOT), F32),
            pltpu.VMEM((4, 4, MSG, 128), F32),
            pltpu.VMEM((4, 4, 32, 128), F32),
            pltpu.VMEM((16, MSG, 128), F32),
            pltpu.VMEM((16, 32, 128), F32),
            pltpu.VMEM((4, 64, 128), F32),
            pltpu.VMEM((128, 8 * RECV), F32),
            pltpu.VMEM((128, 8 * SHOT), F32),
            pltpu.VMEM((8, SMSG, 128), F32),
            pltpu.VMEM((8, RMSG, 128), F32),
            pltpu.VMEM((8, SMSG, 128), F32),
            pltpu.VMEM((RMSG, 128), F32),
            dma((rows // TILE,)),
            dma((4,)),
            dma((2,)),
            dma((16,)), dma((16,)),
            dma((4,)), dma((4,)),
            dma((16,)), dma((16,)),
            dma((7,)), dma((7,)),
            dma((7,)), dma((7,)),
            dma((7,)), dma((7,)),
            dma((10,)), dma((10,)),
            dma((10,)), dma((10,)),
            dma((10,)), dma((10,)),
            dma((10,)), dma((10,)),
        ],
        compiler_params=pltpu.CompilerParams(
            collective_id=0, has_side_effects=True, vmem_limit_bytes=32 * 2**20
        ),
        cost_estimate=pl.CostEstimate(
            flops=9 * 10**9, bytes_accessed=16 * 10**6, transcendentals=2 * 10**6
        ),
    )(shot_id, recv_id, counts, samples, basis)


def residual_kernel(shot_owner, recv_owner, spec, w, table_s, table_r, out, shot_out, recv_out, t):
    step = pl.program_id(0)
    d, side, group, core = place()
    s = 2 * side + core
    width = 4 * RECV

    @pl.when(step == 0)
    def _():
        def put(first, value):
            hi, lo = split(value)
            t[first : first + value.shape[0], 0:width] = hi
            t[first : first + value.shape[0], width : 2 * width] = lo

        for k in range(4):
            terms = [table_r[k % 2, k // 2, j + core, 0:RECV] for j in range(4)]
            put(128 * k, jnp.transpose(jnp.concatenate(terms, axis=0)))
        ends = [table_r[0, 0, j + core, RECV:RMSG] for j in range(4)]
        lines = [ends[j] + pltpu.roll(ends[j + 1], RECV, 1) for j in range(0, 4, 2)]
        put(512, jnp.concatenate(lines, axis=1))

        blank = jnp.zeros((120, 128), F32)
        ends_s = jnp.transpose(jnp.concatenate([table_s[0, 0, 2, SHOT:SMSG], blank], axis=0))
        ends_r = jnp.transpose(jnp.concatenate([table_r[0, 0, 2, RECV:RMSG], blank], axis=0))
        for owner, owned, table, ends, dst in (
            (shot_owner, 8, table_s, ends_s, shot_out),
            (recv_owner, 16, table_r, ends_r, recv_out),
        ):
            top = pl.multiple_of(owned * s, 8)
            index = lax.broadcasted_iota(jnp.int32, (owned, 1), 0)
            pieces = [table[k % 2, k // 2, 2, pl.ds(top, owned)] for k in range(4)]
            end = jnp.zeros((owned, 128), F32)
            for st in range(4):
                end = jnp.where(s == st, ends[owned * st : owned * st + owned], end)
            pieces.append(end)
            for k in range(5):
                value = jnp.zeros((owned, 128), F32)
                for i in range(owned):
                    row = owner[owned * d + i] - owned * d
                    value = jnp.where(index == row, pieces[k][i : i + 1], value)
                if k < 4:
                    dst[:, 128 * k : 128 * k + 128] = value
                else:
                    dst[:, 512:513] = value[:, 0:1]

    part = pl.ds(pl.multiple_of(step * LANES, LANES), LANES)
    hot = w[4 * SHOT :, part]
    terms = jnp.dot(t[...], jnp.concatenate([hot, hot], axis=0), preferred_element_type=F32)
    out[...] = (spec[:, part] - terms)[0 : out.shape[0]]


def residuals(shot_owner, recv_owner, spec, w, table_s, table_r):
    rows = spec.shape[1]
    smem = pl.BlockSpec(memory_space=pltpu.SMEM)
    vmem = pl.BlockSpec(memory_space=pltpu.VMEM)
    return pl.pallas_call(
        residual_kernel,
        grid=(rows // LANES,),
        out_shape=(
            jax.ShapeDtypeStruct((513, rows), F32),
            jax.ShapeDtypeStruct((8, 513), F32),
            jax.ShapeDtypeStruct((16, 513), F32),
        ),
        in_specs=[smem, smem, vmem, vmem, vmem, vmem],
        out_specs=(
            pl.BlockSpec((513, LANES), lambda i: (0, i)),
            pl.BlockSpec((8, 513), lambda i: (0, 0)),
            pl.BlockSpec((16, 513), lambda i: (0, 0)),
        ),
        scratch_shapes=[pltpu.VMEM((spec.shape[0], 8 * RECV), BF16)],
        compiler_params=pltpu.CompilerParams(vmem_limit_bytes=24 * 2**20),
        cost_estimate=pl.CostEstimate(
            flops=3 * 10**9, bytes_accessed=10 * 10**6, transcendentals=0
        ),
    )(shot_owner, recv_owner, spec, w, table_s, table_r)


def shards(basis, odd, samples, shot_id, recv_id, shot_owner, recv_owner, counts):
    rows = samples.shape[0]
    shot_id, recv_id = shot_id.reshape(1, rows), recv_id.reshape(1, rows)
    shot_id, recv_id, samples, basis = (
        pltpu.with_memory_space_constraint(a, pltpu.HBM) for a in (shot_id, recv_id, samples, basis)
    )
    spec, w, table_s, table_r = solve(basis, odd, shot_id, recv_id, counts, samples)
    residual, shots, recvs = residuals(shot_owner, recv_owner, spec, w, table_s, table_r)
    return shots, recvs, residual.T


def solution(mesh):
    basis, odd = basis_table(1024)

    def run(*args):
        return shards(jnp.asarray(basis), odd, *args)

    return jax.shard_map(
        run,
        mesh=mesh,
        in_specs=(
            P(("tile", "block"), None),
            P(("tile", "block")),
            P(("tile", "block")),
            P(),
            P(),
            P(("tile", "block")),
        ),
        out_specs=(
            P(("tile", "block"), None),
            P(("tile", "block"), None),
            P(("tile", "block"), None),
        ),
        check_vma=False,
    )
```

```python
import functools
import math

import jax
import jax.numpy as jnp
import ml_dtypes
import numpy as np
from jax import lax
from jax.experimental import pallas as pl
from jax.experimental.pallas import tpu as pltpu
from jax.sharding import PartitionSpec as P

FLOOR = 0.05
DAMP = 1.0

GROUPS = 32
SHOT = 32
RECV = 64
REACH = 3
MSG = SHOT + RECV + 8
SMSG = SHOT + 8
RMSG = RECV + 8
TILE = 1024
LANES = 1024
MESH = pl.DeviceIdType.MESH
F32 = jnp.float32
BF16 = jnp.bfloat16
HIGH = lax.Precision.HIGHEST
NT = (((1,), (1,)), ((), ()))


def basis_table(nsamp):
    half = nsamp // 2
    freq = np.arange(half + 1, dtype=np.int64)
    sample = np.arange(nsamp, dtype=np.int64)
    phase = sample[:, None] * freq[None, :] % nsamp
    angle = phase.astype(np.float32) * np.float32(2.0 * math.pi / nsamp)
    norm = np.float32(1.0 / math.sqrt(nsamp))
    cos = (np.cos(angle) * norm).astype(ml_dtypes.bfloat16)
    sin = (-np.sin(angle) * norm).astype(ml_dtypes.bfloat16)
    odd = float(sin[1, half])
    parts = []
    for k in range(0, half, 128):
        parts += [cos[:, k : k + 128], sin[:, k : k + 128]]
    return np.concatenate(parts, axis=1), (odd, float(norm))


def place():
    d = lax.axis_index("tile") * 32 + lax.axis_index("block")
    return d, d // 64, (d % 64) // 2, d % 2


def device(side, group, core):
    return side * 64 + 2 * lax.rem(group + GROUPS, GROUPS) + core


def coords(d):
    return (d // 32, lax.rem(d, 32))


def local_rows(ident, live, group, core, owned):
    half = owned // 2
    total = half * GROUPS
    side = ident // total
    within = ident & (total - 1)
    j = (within // half - (group - 2 + core) + 2 * GROUPS) & (GROUPS - 1)
    row = side * half + (within & (half - 1))
    return jnp.where(live, j, -1), row


def split(x):
    hi = x.astype(BF16)
    return hi, (x - hi.astype(F32)).astype(BF16)


def solve_kernel(
    odd, shot_ref, recv_ref, count_ref, samples, basis, spec, w, table_s, table_r,
    x, b, shot_ids, recv_ids, hl, acc, cacc, racc, msgs, cmsg, inbox, cin, cg, csr, crs,
    s1, r1, s2, r2, in_sem, b_sem, id_sem, c_send, c_recv, g_send, g_recv,
    p_send, p_recv, s1_send, s1_recv, r1_send, r1_recv, s2_send, s2_recv,
    ts_send, ts_recv, tr_send, tr_recv, fs_send, fs_recv, fr_send, fr_recv,
):
    me, side, group, core = place()
    s = 2 * side + core
    rows = x.shape[0]
    tiles = rows // TILE

    sides, cores = (side, 1 - side), (core, 1 - core)
    places = {}
    for off in range(-REACH, REACH + 1):
        g = lax.rem(group + (off + GROUPS), GROUPS)
        places[off] = (g // 16, 2 * lax.rem(g, 16))
    far_off = 4 * core - 2
    g = lax.rem(group + far_off + GROUPS, GROUPS)
    places["far"] = (g // 16, 2 * lax.rem(g, 16))

    def peer(off, r):
        tile, block = places[off]
        return (2 * sides[r // 2] + tile, block + cores[r % 2])

    def edge_peer(off, r1):
        tile, block = places[off]
        return (2 * sides[r1] + tile, block + (0 if off > 0 else 1))

    window = ((0, 2 - core), (-1, 1 - core), (1, 3 - core), ("far", 3 * core))

    def landing(off, r):
        if off == "far":
            return 12 + 2 * core + r // 2
        return {0: r, 1: 4 + r, -1: 8 + r}[off]

    def remote(src, dst, send, recv, target):
        return pltpu.make_async_remote_copy(
            src_ref=src, dst_ref=dst, send_sem=send, recv_sem=recv,
            device_id=target, device_id_type=MESH,
        )

    barrier = pltpu.get_barrier_semaphore()
    near = [peer(off, r) for off in range(-2, 3) for r in range(4) if (off, r) != (0, 0)]
    for target in near + [peer(-REACH, 0), peer(REACH, 0)]:
        pl.semaphore_signal(barrier, inc=1, device_id=target, device_id_type=MESH)

    def quarter(r):
        return 2 * sides[r // 2] + cores[r % 2]

    def load(i):
        part = pl.ds(pl.multiple_of(i * TILE, TILE), TILE)
        return pltpu.make_async_copy(samples.at[part], x.at[part], in_sem.at[i])

    def load_basis(n, r):
        part = pl.ds(pl.multiple_of(256 * quarter(r), 256), 256)
        return pltpu.make_async_copy(basis.at[:, part], b.at[n], b_sem.at[n])

    ids = [
        pltpu.make_async_copy(shot_ref, shot_ids, id_sem.at[0]),
        pltpu.make_async_copy(recv_ref, recv_ids, id_sem.at[1]),
    ]
    for copy in ids:
        copy.start()
    order = (3, 2, 1, 0)
    load_basis(0, order[0]).start()
    for i in range(tiles):
        load(i).start()
    for n in range(1, 4):
        load_basis(n, order[n]).start()

    for copy in ids:
        copy.wait()
    slot = lax.broadcasted_iota(jnp.int32, (1, rows), 1)
    live = slot < count_ref[0]
    sj, srow = local_rows(shot_ids[...], live, group, core, SHOT)
    rj, rrow = local_rows(recv_ids[...], live, group, core, RECV)
    srow = jnp.where(live, sj * SHOT + srow, -1)
    rrow = jnp.where(live, rj * RECV + rrow, -1)
    for i in range(tiles):
        cols = slice(i * TILE, (i + 1) * TILE)
        ident = lax.broadcasted_iota(jnp.int32, (4 * SHOT, TILE), 0)
        w[: 4 * SHOT, cols] = (ident == srow[:, cols]).astype(F32).astype(BF16)
        ident = lax.broadcasted_iota(jnp.int32, (4 * RECV, TILE), 0)
        w[4 * SHOT :, cols] = (ident == rrow[:, cols]).astype(F32).astype(BF16)
    cacc[...] = jnp.zeros_like(cacc)
    racc[...] = jnp.zeros_like(racc)

    def tally(i, _):
        part = pl.ds(pl.multiple_of(i * TILE, TILE), TILE)
        ws, wr = w[: 4 * SHOT, part], w[4 * SHOT :, part]
        cacc[...] += lax.dot_general(ws, wr, NT, preferred_element_type=F32)
        racc[...] += lax.dot_general(wr, ws, NT, preferred_element_type=F32)
        return 0

    csr[...] = jnp.zeros_like(csr)
    crs[...] = jnp.zeros_like(crs)

    def count_copy(n):
        (off, j), r = window[n // 4], n % 4
        to = landing(off, r)
        return remote(
            cmsg.at[j, quarter(r)], cin.at[to], c_send.at[n], c_recv.at[to], peer(off, r)
        )

    lane = lax.broadcasted_iota(jnp.int32, (TILE, 128), 1)
    lane8 = lax.broadcasted_iota(jnp.int32, (8, 128), 1)
    sine, norm = odd

    def nyquist(i):
        part = slice(i * TILE, (i + 1) * TILE)
        even_odd = x[part, 0:128].astype(F32)
        for v in range(1, x.shape[1] // 128):
            even_odd += x[part, 128 * v : 128 * v + 128].astype(F32)
        odds = jnp.sum(jnp.where(lane % 2 == 1, even_odd, 0.0), axis=1, keepdims=True)
        evens = jnp.sum(jnp.where(lane % 2 == 1, 0.0, even_odd), axis=1, keepdims=True)
        re, im = (evens - odds) * norm, odds * sine
        return jnp.log(jnp.broadcast_to(re * re + im * im, (TILE, 128)) + FLOOR)

    def log_spectra(n):
        load_basis(n, order[n]).wait()
        first = pl.multiple_of(128 * quarter(order[n]), 128)
        for i in range(tiles):
            if n == 0:
                load(i).wait()
            part = slice(i * TILE, (i + 1) * TILE)
            y = jnp.dot(x[part], b[n], preferred_element_type=F32)
            re, im = y[:, :128], y[:, 128:]
            value = jnp.log(re * re + im * im + FLOOR)
            spec[pl.ds(first, 128), part] = jnp.transpose(value)
            hl[part, 0:128], hl[part, 128:256] = split(value)
            if n == 0:
                value = nyquist(i)
                spec[512:520, part] = jnp.transpose(value)[0:8]
                hi, lo = split(value)
                hl[part, 256:384] = jnp.where(lane == 0, hi.astype(F32), lo.astype(F32)).astype(BF16)
        width = 384 if n == 0 else 256
        acc[:, :width] = jnp.dot(w[...], hl[:, :width], preferred_element_type=F32)
        for j in range(4):
            for top, size, to in ((j * SHOT, SHOT, 0), (4 * SHOT + j * RECV, RECV, SHOT)):
                msgs[n, j, to : to + size] = (
                    acc[top : top + size, 0:128] + acc[top : top + size, 128:256]
                )
        if n == 0:
            both = acc[:, 256:384]
            both = both + pltpu.roll(both, 127, 1)
            line = [
                jnp.broadcast_to(jnp.transpose(both[128 * v : 128 * v + 128])[0:1], (8, 128))
                for v in range(3)
            ]
            for j in range(4):
                shots = pltpu.roll(line[0], (128 - SHOT * j) % 128, 1)
                recvs = pltpu.roll(line[1 + j // 2], (SHOT + 128 - RECV * (j % 2)) % 128, 1)
                ends = jnp.where(lane8 < SHOT, shots, recvs)
                ends = jnp.where(lane8 < SHOT + RECV, ends, 0.0)
                for m in range(4):
                    msgs[m, j, SHOT + RECV : MSG] = ends

    def sum_copy(n, which):
        (off, j), r = window[which], order[n]
        to = landing(off, r)
        return remote(
            msgs.at[n, j], inbox.at[to], p_send.at[4 * n + which], p_recv.at[to], peer(off, r)
        )

    def sum_copies(n):
        return [sum_copy(n, which) for which in range(4) if (which, order[n]) != (0, 0)]

    def send_sums(n):
        for copy in sum_copies(n):
            copy.start()
        if order[n] == 0:
            inbox[0] = msgs[n, 2 - core]

    def senders():
        yield from ((r, peer(0, r)) for r in range(1, 4))
        for base, off in ((4, -1), (8, 1)):
            yield from ((base + r, peer(off, r)) for r in range(4))
        for base, off in ((12, 2), (14, -2)):
            yield from ((base + r1, edge_peer(off, r1)) for r1 in range(2))

    def arrived(buf, send, recv):
        for n, source in senders():
            remote(buf.at[n], buf.at[n], send.at[n], recv.at[n], source).wait_recv()

    def member_copy(r):
        return remote(cg.at[s], cg.at[s], g_send.at[r], g_recv.at[r], peer(0, r))

    def share_counts():
        arrived(cin, c_send, c_recv)
        shots = jnp.zeros((8, 512), F32)
        recvs = jnp.zeros((16, 256), F32)
        for place in range(4):
            far = {0: 14, 3: 12}
            if place in far:
                base, c = (4, core) if place == 0 else (8, 1 - core)
                part = cin[far[place]] + cin[far[place] + 1]
                part = part + cin[base + c] + cin[base + 2 + c]
            else:
                low, high = (4, 0) if place == 1 else (0, 8)
                part = cin[low + 1 - core] + cin[low + 3 - core]
                part = part + cin[high + core] + cin[high + 2 + core]
            wide = jnp.concatenate([part[0:8], part[8:16], jnp.zeros((8, 256), F32)], axis=1)
            shots += pltpu.roll(wide, RECV * place, 1) if place else wide
            wide = jnp.concatenate([part[16:32], jnp.zeros((16, 128), F32)], axis=1)
            recvs += pltpu.roll(wide, SHOT * place, 1) if place else wide
        for v in range(4):
            cg[s, 8 * v : 8 * v + 8] = shots[:, 128 * v : 128 * v + 128]
        for v in range(2):
            cg[s, 32 + 16 * v : 48 + 16 * v] = recvs[:, 128 * v : 128 * v + 128]
        for r in range(1, 4):
            member_copy(r).start()

    def take_counts():
        for r in range(1, 4):
            st = quarter(r)
            remote(cg.at[st], cg.at[st], g_send.at[r], g_recv.at[r], peer(0, r)).wait_recv()
        for st in range(4):
            for v in range(4):
                csr[8 * st : 8 * st + 8, 128 * v : 128 * v + 128] = cg[st, 8 * v : 8 * v + 8]
            for v in range(2):
                crs[16 * st : 16 * st + 16, 128 * v : 128 * v + 128] = cg[
                    st, 32 + 16 * v : 48 + 16 * v
                ]

    log_spectra(0)
    lax.fori_loop(0, tiles, tally, 0)
    for j in range(4):
        for st in range(4):
            top = j * SHOT + 8 * st
            cmsg[j, st, 0:8] = cacc[top : top + 8, 0:128]
            cmsg[j, st, 8:16] = cacc[top : top + 8, 128:256]
            top = j * RECV + 16 * st
            cmsg[j, st, 16:32] = racc[top : top + 16, :]
    pl.semaphore_wait(barrier, 21)
    for n in range(1, 16):
        count_copy(n).start()
    cin[0] = cmsg[2 - core, s]
    send_sums(0)
    log_spectra(1)
    send_sums(1)
    log_spectra(2)
    send_sums(2)
    share_counts()
    log_spectra(3)
    send_sums(3)
    take_counts()

    shot_counts = jnp.sum(csr[0:SHOT], axis=1, keepdims=True) + DAMP
    recv_counts = jnp.sum(crs[0:RECV], axis=1, keepdims=True) + DAMP

    def matmul(p, q):
        return jnp.dot(p, q, precision=HIGH, preferred_element_type=F32)

    def matmul_nt(p, q):
        return lax.dot_general(p, q, NT, precision=HIGH, preferred_element_type=F32)

    shot_line = matmul_nt(jnp.ones((8, 512), F32), csr[...]) + DAMP
    recv_line = matmul_nt(jnp.ones((8, 256), F32), crs[...]) + DAMP
    for buf, size in ((s1, SMSG), (r1, RMSG), (s2, SMSG)):
        buf[7] = jnp.zeros((size, 128), F32)

    arrived(inbox, p_send, p_recv)
    total = inbox[0]
    for n in range(1, 16):
        total = total + inbox[n]
    shot_sum = total[0:SHOT]
    recv_sum = total[SHOT : SHOT + RECV]
    ends = total[SHOT + RECV : MSG]
    shot_end = jnp.where(lane8 < SHOT, ends, 0.0)
    recv_end = jnp.where(lane8 < RECV, pltpu.roll(ends, 128 - SHOT, 1), 0.0)

    def spread_copy(buf, send, recv, off):
        return remote(
            buf.at[3], buf.at[3 - off], send.at[3 - off], recv.at[3 - off], peer(off, 0)
        )

    offsets = (3, -3, 2, -2, 1, -1)

    def spread(buf, send, recv):
        for off in offsets:
            spread_copy(buf, send, recv, off).start()

    def gathered(buf, send, recv):
        for off in offsets:
            spread_copy(buf, send, recv, off).wait_recv()

    def shot_matrix(buf):
        main = buf[:, 0:SHOT].reshape(8 * SHOT, 128)
        line = [jnp.zeros((8, 128), F32) for _ in range(2)]
        for n in range(7):
            piece = buf[n, SHOT:SMSG]
            line[n // 4] += pltpu.roll(piece, SHOT * (n % 4), 1) if n % 4 else piece
        return main, jnp.concatenate(line, axis=1)

    def recv_matrix(buf):
        main = buf[:, 0:RECV].reshape(8 * RECV, 128)
        line = [jnp.zeros((8, 128), F32) for _ in range(4)]
        for n in range(7):
            piece = buf[n, RECV:RMSG]
            line[n // 2] += pltpu.roll(piece, RECV, 1) if n % 2 else piece
        return main, jnp.concatenate(line, axis=1)

    s1[3, 0:SHOT] = shot_sum / shot_counts
    s1[3, SHOT:SMSG] = shot_end / shot_line
    spread(s1, s1_send, s1_recv)
    gathered(s1, s1_send, s1_recv)

    main, line = shot_matrix(s1)
    r1[3, 0:RECV] = (recv_sum - matmul(crs[0:RECV], main)) / recv_counts
    r1[3, RECV:RMSG] = (recv_end - matmul_nt(line, crs[...])) / recv_line
    spread(r1, r1_send, r1_recv)
    gathered(r1, r1_send, r1_recv)

    main, line = recv_matrix(r1)
    s2[3, 0:SHOT] = (shot_sum - matmul(csr[0:SHOT], main)) / shot_counts
    s2[3, SHOT:SMSG] = (shot_end - matmul_nt(line, csr[...])) / shot_line
    spread(s2, s2_send, s2_recv)

    def publications(src, table, send, recv):
        for off in (2, -2, 1, -1, 0):
            for r in (2, 0):
                if (off, r) != (0, 0):
                    n = 5 * (r // 2) + 2 - off
                    yield remote(
                        src, table.at[core, side, 2 - off], send.at[n], recv.at[n], peer(off, r)
                    )

    def hand_on(table, send, recv, r, off):
        n = 5 * (r // 2) + 2 + off
        block = table.at[core, sides[r // 2], 2 + off]
        return remote(block, block, send.at[n], recv.at[n], peer(0, 1))

    def relay(src, table, send, recv, send_on, recv_on):
        for r in (0, 2):
            for off in (0, 1, -1, 2, -2):
                if (off, r) != (0, 0):
                    n = 5 * (r // 2) + 2 + off
                    remote(
                        src, table.at[core, sides[r // 2], 2 + off], send.at[n], recv.at[n],
                        peer(off, r),
                    ).wait_recv()
                hand_on(table, send_on, recv_on, r, off).start()

    def relayed(table, send, recv):
        for r in (0, 2):
            for off in (0, 1, -1, 2, -2):
                n = 5 * (r // 2) + 2 + off
                block = table.at[1 - core, sides[r // 2], 2 + off]
                remote(block, block, send.at[n], recv.at[n], peer(0, 1)).wait_recv()

    shot_terms = (s2.at[3], table_s, ts_send, ts_recv)
    recv_terms = (r2, table_r, tr_send, tr_recv)

    def publish(*what):
        for copy in publications(*what):
            copy.start()

    publish(*shot_terms)
    table_s[core, side, 2] = s2[3]
    gathered(s2, s2_send, s2_recv)

    main, line = shot_matrix(s2)
    r2[0:RECV] = (recv_sum - matmul(crs[0:RECV], main)) / recv_counts
    r2[RECV:RMSG] = (recv_end - matmul_nt(line, crs[...])) / recv_line
    publish(*recv_terms)
    table_r[core, side, 2] = r2[...]

    relay(*shot_terms, fs_send, fs_recv)
    relayed(table_s, fs_send, fs_recv)

    def both_parts(value):
        return jnp.concatenate(split(value), axis=1)

    lifted = []
    for k in range(4):
        terms = jnp.concatenate([table_s[k % 2, k // 2, j + core, 0:SHOT] for j in range(4)], axis=0)
        lifted.append(both_parts(jnp.transpose(terms)))
    line = table_s[0, 0, core, SHOT:SMSG]
    for j in range(1, 4):
        line = line + pltpu.roll(table_s[0, 0, j + core, SHOT:SMSG], SHOT * j, 1)
    lifted.append(both_parts(line))
    for i in range(tiles):
        part = slice(i * TILE, (i + 1) * TILE)
        hot = jnp.concatenate([w[0 : 4 * SHOT, part]] * 2, axis=0)
        for k in range(5):
            bins = slice(128 * k, min(128 * k + 128, spec.shape[0]))
            terms = jnp.dot(lifted[k], hot, preferred_element_type=F32)
            spec[bins, part] = jnp.where(live[:, part], spec[bins, part], 0.0) - terms

    for n in range(1, 16):
        count_copy(n).wait_send()
    for n in range(4):
        for copy in sum_copies(n):
            copy.wait_send()
    for r in range(1, 4):
        member_copy(r).wait_send()
    for off in offsets:
        spread_copy(s1, s1_send, s1_recv, off).wait_send()
        spread_copy(r1, r1_send, r1_recv, off).wait_send()
        spread_copy(s2, s2_send, s2_recv, off).wait_send()
    for what in (shot_terms, recv_terms):
        for copy in publications(*what):
            copy.wait_send()
    relay(*recv_terms, fr_send, fr_recv)
    for r in (0, 2):
        for off in range(-2, 3):
            hand_on(table_s, fs_send, fs_recv, r, off).wait_send()
            hand_on(table_r, fr_send, fr_recv, r, off).wait_send()
    relayed(table_r, fr_send, fr_recv)


def solve(basis, odd, shot_id, recv_id, counts, samples):
    rows, nsamp = samples.shape
    dma = pltpu.SemaphoreType.DMA
    vmem = pl.BlockSpec(memory_space=pltpu.VMEM)
    hbm = pl.BlockSpec(memory_space=pltpu.HBM)
    return pl.pallas_call(
        functools.partial(solve_kernel, odd),
        out_shape=(
            jax.ShapeDtypeStruct((nsamp // 2 + 8, rows), F32),
            jax.ShapeDtypeStruct((4 * (SHOT + RECV), rows), BF16),
            jax.ShapeDtypeStruct((2, 2, 5, SMSG, 128), F32),
            jax.ShapeDtypeStruct((2, 2, 5, RMSG, 128), F32),
        ),
        in_specs=[hbm, hbm, pl.BlockSpec(memory_space=pltpu.SMEM), hbm, hbm],
        out_specs=(vmem, vmem, vmem, vmem),
        scratch_shapes=[
            pltpu.VMEM((rows, nsamp), BF16),
            pltpu.VMEM((4, nsamp, 256), BF16),
            pltpu.VMEM((1, rows), jnp.int32),
            pltpu.VMEM((1, rows), jnp.int32),
            pltpu.VMEM((rows, 384), BF16),
            pltpu.VMEM((4 * (SHOT + RECV), 384), F32),
            pltpu.VMEM((4 * SHOT, 4 * RECV), F32),
            pltpu.VMEM((4 * RECV, 4 * SHOT), F32),
            pltpu.VMEM((4, 4, MSG, 128), F32),
            pltpu.VMEM((4, 4, 32, 128), F32),
            pltpu.VMEM((16, MSG, 128), F32),
            pltpu.VMEM((16, 32, 128), F32),
            pltpu.VMEM((4, 64, 128), F32),
            pltpu.VMEM((128, 8 * RECV), F32),
            pltpu.VMEM((128, 8 * SHOT), F32),
            pltpu.VMEM((8, SMSG, 128), F32),
            pltpu.VMEM((8, RMSG, 128), F32),
            pltpu.VMEM((8, SMSG, 128), F32),
            pltpu.VMEM((RMSG, 128), F32),
            dma((rows // TILE,)),
            dma((4,)),
            dma((2,)),
            dma((16,)), dma((16,)),
            dma((4,)), dma((4,)),
            dma((16,)), dma((16,)),
            dma((7,)), dma((7,)),
            dma((7,)), dma((7,)),
            dma((7,)), dma((7,)),
            dma((10,)), dma((10,)),
            dma((10,)), dma((10,)),
            dma((10,)), dma((10,)),
            dma((10,)), dma((10,)),
        ],
        compiler_params=pltpu.CompilerParams(
            collective_id=0, has_side_effects=True, vmem_limit_bytes=32 * 2**20
        ),
        cost_estimate=pl.CostEstimate(
            flops=9 * 10**9, bytes_accessed=16 * 10**6, transcendentals=2 * 10**6
        ),
    )(shot_id, recv_id, counts, samples, basis)


def residual_kernel(shot_owner, recv_owner, spec, w, table_s, table_r, out, shot_out, recv_out, t):
    step = pl.program_id(0)
    d, side, group, core = place()
    s = 2 * side + core
    width = 4 * RECV

    @pl.when(step == 0)
    def _():
        def put(first, value):
            hi, lo = split(value)
            t[first : first + value.shape[0], 0:width] = hi
            t[first : first + value.shape[0], width : 2 * width] = lo

        for k in range(4):
            terms = [table_r[k % 2, k // 2, j + core, 0:RECV] for j in range(4)]
            put(128 * k, jnp.transpose(jnp.concatenate(terms, axis=0)))
        ends = [table_r[0, 0, j + core, RECV:RMSG] for j in range(4)]
        lines = [ends[j] + pltpu.roll(ends[j + 1], RECV, 1) for j in range(0, 4, 2)]
        put(512, jnp.concatenate(lines, axis=1))

        blank = jnp.zeros((120, 128), F32)
        ends_s = jnp.transpose(jnp.concatenate([table_s[0, 0, 2, SHOT:SMSG], blank], axis=0))
        ends_r = jnp.transpose(jnp.concatenate([table_r[0, 0, 2, RECV:RMSG], blank], axis=0))
        for owner, owned, table, ends, dst in (
            (shot_owner, 8, table_s, ends_s, shot_out),
            (recv_owner, 16, table_r, ends_r, recv_out),
        ):
            top = pl.multiple_of(owned * s, 8)
            index = lax.broadcasted_iota(jnp.int32, (owned, 1), 0)
            pieces = [table[k % 2, k // 2, 2, pl.ds(top, owned)] for k in range(4)]
            end = jnp.zeros((owned, 128), F32)
            for st in range(4):
                end = jnp.where(s == st, ends[owned * st : owned * st + owned], end)
            pieces.append(end)
            for k in range(5):
                value = jnp.zeros((owned, 128), F32)
                for i in range(owned):
                    row = owner[owned * d + i] - owned * d
                    value = jnp.where(index == row, pieces[k][i : i + 1], value)
                if k < 4:
                    dst[:, 128 * k : 128 * k + 128] = value
                else:
                    dst[:, 512:513] = value[:, 0:1]

    part = pl.ds(pl.multiple_of(step * LANES, LANES), LANES)
    hot = w[4 * SHOT :, part]
    terms = jnp.dot(t[...], jnp.concatenate([hot, hot], axis=0), preferred_element_type=F32)
    out[...] = (spec[:, part] - terms)[0 : out.shape[0]]


def residuals(shot_owner, recv_owner, spec, w, table_s, table_r):
    rows = spec.shape[1]
    smem = pl.BlockSpec(memory_space=pltpu.SMEM)
    vmem = pl.BlockSpec(memory_space=pltpu.VMEM)
    return pl.pallas_call(
        residual_kernel,
        grid=(rows // LANES,),
        out_shape=(
            jax.ShapeDtypeStruct((513, rows), F32),
            jax.ShapeDtypeStruct((8, 513), F32),
            jax.ShapeDtypeStruct((16, 513), F32),
        ),
        in_specs=[smem, smem, vmem, vmem, vmem, vmem],
        out_specs=(
            pl.BlockSpec((513, LANES), lambda i: (0, i)),
            pl.BlockSpec((8, 513), lambda i: (0, 0)),
            pl.BlockSpec((16, 513), lambda i: (0, 0)),
        ),
        scratch_shapes=[pltpu.VMEM((spec.shape[0], 8 * RECV), BF16)],
        compiler_params=pltpu.CompilerParams(vmem_limit_bytes=24 * 2**20),
        cost_estimate=pl.CostEstimate(
            flops=3 * 10**9, bytes_accessed=10 * 10**6, transcendentals=0
        ),
    )(shot_owner, recv_owner, spec, w, table_s, table_r)


def shards(basis, odd, samples, shot_id, recv_id, shot_owner, recv_owner, counts):
    rows = samples.shape[0]
    shot_id, recv_id = shot_id.reshape(1, rows), recv_id.reshape(1, rows)
    shot_id, recv_id, samples, basis = (
        pltpu.with_memory_space_constraint(a, pltpu.HBM) for a in (shot_id, recv_id, samples, basis)
    )
    spec, w, table_s, table_r = solve(basis, odd, shot_id, recv_id, counts, samples)
    residual, shots, recvs = residuals(shot_owner, recv_owner, spec, w, table_s, table_r)
    return shots, recvs, residual.T


def solution(mesh):
    basis, odd = basis_table(1024)

    def run(*args):
        return shards(jnp.asarray(basis), odd, *args)

    return jax.shard_map(
        run,
        mesh=mesh,
        in_specs=(
            P(("tile", "block"), None),
            P(("tile", "block")),
            P(("tile", "block")),
            P(),
            P(),
            P(("tile", "block")),
        ),
        out_specs=(
            P(("tile", "block"), None),
            P(("tile", "block"), None),
            P(("tile", "block"), None),
        ),
        check_vma=False,
    )
```
